512 devices in a mesh: section: 8 (over x, core), group: 4 (over z_hi), tp: 16 (over y, z_lo).
Axes of the slice: x: 4, y: 8, z: 8 (z_hi: 4, z_lo: 2; z = z_hi * 2 + z_lo), core: 2. Of those that a mesh axis runs over, the one named last changes fastest.
Arguments:
- vision_hidden: bfloat16 [8192, 8192], P(('section', 'group'), 'tp'), may hold values from -6 to 6
- proj_weight: bfloat16 [8192, 8192], P('group', 'tp'), may hold values from -0.0625 to 0.0625
- proj_bias: bfloat16 [8192], P('tp'), may hold values from -3 to 3
- text_embed: bfloat16 [32768, 8192], P(('section', 'group'), 'tp')
- norm_gain: float32 [8192], P('tp'), may hold values from 0.1 to 1.9
- key_weight: bfloat16 [8192, 1024], P('tp'), may hold values from -0.0625 to 0.0625
- image_group: int32 [32], replicated, may hold values from 0 to 3, as said below
- image_offset: int32 [32], replicated, may hold values from 0 to 768, as said below
Outputs:
- keys: bfloat16 [32768, 1024], P(('section', 'group', 'tp'))
The draws below stay inside these ranges and needn't reach their ends.
Inputs may be any that keep to these rules, and one draw needn't show every extreme that they name: `image_group`: of the 4 images of one section, exactly two name the same group and the others name distinct other groups. `image_offset`: each image slot lies inside its prompt, and the two slots that share a prompt do not intersect.
All inputs are finite; a program needn't handle non-finite values.
Results may differ from the reference program's by a relative error of at most 0.0052.
Values may be sent and summed in bfloat16 or wider, within the bound.
A program may use at most 64 MiB of HBM per device.

```python
import jax
import jax.numpy as jnp
from jax import lax

D = 8192
KV_W = 1024
IMG_TOK = 256
PROMPT = 1024
IMAGES = 32
ROWS = 32768
N_SECTION = 8
N_GROUP = 4


def slot_plan(key):
    keys = jax.random.split(key, 5)
    perms = jax.vmap(lambda k: jax.random.permutation(k, N_GROUP))(jax.random.split(keys[0], N_SECTION))
    targets = jnp.concatenate([perms[:, :1], perms[:, :N_GROUP - 1]], axis=1)
    order = jax.vmap(lambda k: jax.random.permutation(k, N_GROUP))(jax.random.split(keys[1], N_SECTION))
    first = jax.random.randint(keys[2], (N_SECTION, 1), 0, PROMPT - 2 * IMG_TOK + 1)
    second = first + IMG_TOK + jax.random.randint(keys[3], (N_SECTION, 1), 0, PROMPT - 2 * IMG_TOK + 1 - first)
    leading = (jnp.arange(N_SECTION) == 0)[:, None]
    first = jnp.where(leading, 0, first)
    second = jnp.where(leading, PROMPT - IMG_TOK, second)
    single = jax.random.randint(keys[4], (N_SECTION, N_GROUP - 2), 0, PROMPT - IMG_TOK + 1)
    starts = jnp.concatenate([first, second, single], axis=1)
    group = jnp.take_along_axis(targets, order, axis=1).reshape(-1)
    offset = jnp.take_along_axis(starts, order, axis=1).reshape(-1)
    return (group.astype(jnp.int32), offset.astype(jnp.int32))


def draw_image_group(key, part):
    plan = slot_plan(key)
    return plan[0]


def draw_image_offset(key, part):
    plan = slot_plan(key)
    return plan[1]


def draw_text_embed(key, part):
    key = jax.random.fold_in(key, 11)
    keys = jax.random.split(key, 3)
    base = jax.random.normal(keys[0], (ROWS, D), jnp.float32)
    row_scale = jnp.exp(jax.random.uniform(keys[1], (ROWS, 1), jnp.float32, 0.0, 2.3))
    col_scale = jnp.exp(jax.random.uniform(keys[2], (1, D), jnp.float32, 0.0, 2.3))
    return (base * row_scale * col_scale / 3.0).astype(jnp.bfloat16)


def levels(own_key, dims, cuts, smallest, top_value):
    level = 1.0
    for dim, blocks in cuts:
        steps = jax.random.uniform(jax.random.fold_in(jax.random.fold_in(own_key, 6), dim), (blocks,), jnp.float32, smallest / len(cuts), top_value / len(cuts))
        level = level * jnp.repeat(jnp.exp(steps), dims[dim] // blocks).reshape((-1,) + (1,) * (len(dims) - 1 - dim))
    return level


def noise(stream_key, dims, width, reach, pieces=(), kind=jnp.bfloat16):
    factor_of = levels(stream_key, dims, pieces, -0.22, 0.18) if pieces else 1.0
    entries = jax.random.normal(stream_key, dims, jnp.float32) * width * factor_of
    return jnp.minimum(jnp.maximum(entries, -reach), reach).astype(kind)


def setup_inputs(seed: int = 0) -> dict:
    arg_keys = jax.random.split(jax.random.key(seed), 9)
    vision_hidden = noise(arg_keys[0], (IMAGES * IMG_TOK, D), 1.0, 6.0, ((0, 32), (1, 16)))
    proj_weight = noise(arg_keys[1], (D, D), D ** -0.5, 0.0625, ((0, 4), (1, 16)))
    proj_bias = noise(arg_keys[2], (D,), 0.5, 3.0, ((0, 16),))
    text_embed = draw_text_embed(jax.random.fold_in(arg_keys[8], 71), 0)
    norm_gain = jnp.clip(1.0 + 0.18 * jax.random.normal(arg_keys[4], (D,), jnp.float32), 0.1, 1.9)
    key_weight = noise(arg_keys[5], (D, KV_W), D ** -0.5, 0.0625, ((0, 16),))
    image_group = draw_image_group(jax.random.fold_in(arg_keys[8], 71), 0)
    image_offset = draw_image_offset(jax.random.fold_in(arg_keys[8], 71), 0)
    return {"vision_hidden": vision_hidden, "proj_weight": proj_weight, "proj_bias": proj_bias, "text_embed": text_embed, "norm_gain": norm_gain, "key_weight": key_weight, "image_group": image_group, "image_offset": image_offset}


def reference(vision_hidden, proj_weight, proj_bias, text_embed, norm_gain, key_weight, image_group, image_offset):
    summed = jnp.dot(vision_hidden, proj_weight, preferred_element_type=jnp.float32)
    projected = (summed + proj_bias.astype(jnp.float32)).astype(jnp.bfloat16)
    half = N_SECTION // 2

    def place(index, prompt):
        section_src = index // N_GROUP
        block = (section_src + half) % N_SECTION * N_GROUP + image_group[index]
        start = (block * PROMPT + image_offset[index]).astype(jnp.int32)
        first = (index * IMG_TOK).astype(jnp.int32)
        rows = lax.dynamic_slice_in_dim(projected, first, IMG_TOK, 0)
        return lax.dynamic_update_slice_in_dim(prompt, rows, start, 0)
    prompt = lax.fori_loop(0, N_SECTION * N_GROUP, place, text_embed)
    blocks = prompt.reshape(N_SECTION * N_GROUP, PROMPT, D)

    def encode(block):
        values = block.astype(jnp.float32)
        inv_rms = 1.0 / jnp.sqrt(lax.optimization_barrier(jnp.sum(values * values, axis=1, keepdims=True)) / D + 1e-05)
        normed = (values * inv_rms * norm_gain).astype(jnp.bfloat16)
        return jnp.dot(normed, key_weight, preferred_element_type=jnp.float32).astype(jnp.bfloat16)
    return lax.map(encode, blocks).reshape(ROWS, KV_W)
```

```python
import jax
import jax.numpy as jnp
from jax import lax
from jax.experimental import pallas as pl
from jax.experimental.pallas import tpu as pltpu
from jax.sharding import PartitionSpec as P

MESH = pl.DeviceIdType.MESH
D = 8192
KV = 1024
PAD = 128
WIDE = KV + PAD
EPS = 1e-05
BIG = 1.9e19
F32 = jnp.float32
BF16 = jnp.bfloat16
SEMS = 160


def dot(a, b):
    return jnp.dot(a, b, preferred_element_type=F32)


def three_parts(v):
    lane = lax.broadcasted_iota(jnp.int32, (v.shape[0], PAD), 1)
    hi = v.astype(BF16).astype(F32)
    rest = jnp.where(hi < jnp.inf, v - hi, 0.0)
    mid = rest.astype(BF16).astype(F32)
    low = rest - mid
    parts = jnp.where(lane == 0, hi, jnp.where(lane == 1, mid, jnp.where(lane == 2, low, 0.0)))
    return parts.astype(BF16)


def inverse_rms(half_sum):
    return 1.0 / jnp.sqrt(half_sum * 2.0 / D + EPS)


def kernel(
    vis, wp, bias, txt, gain, kw, grp, off, out,
    xb, wb, tv, kwv, tsend, trecv, town, ysend, yrecv, acc, isend, irecv, ikey, dest, ag,
    ssem, rsem, lsem,
):
    s, g, t = lax.axis_index("section"), lax.axis_index("group"), lax.axis_index("tp")
    y, l = t // 2, t % 2
    other = 1 - l
    partner = 2 * y + other
    sib = s + 1 - 2 * (s % 2)
    g_up, g_down, g_far = (g + 1) % 4, (g + 3) % 4, (g + 2) % 4
    s_up, s_down, s_far = (s + 2) % 8, (s + 6) % 8, (s + 4) % 8

    local = []
    for k, (src, dst) in enumerate(
        ((txt, tv), (kw, kwv), (vis, xb.at[t]), (wp, wb.at[g]))
    ):
        copy = pltpu.make_async_copy(src, dst, lsem.at[k])
        copy.start()
        local.append(copy)

    peers = [{"tp": (t + d) % 16} for d in range(1, 16)]
    peers += [{"group": g_up}, {"group": g_down}]
    peers += [{"section": s_up}, {"section": s_down}, {"section": sib}]
    peers += [{"section": s_far, "group": h} for h in range(4)]
    barrier = pltpu.get_barrier_semaphore()
    for peer in peers:
        pl.semaphore_signal(barrier, inc=1, device_id=peer, device_id_type=MESH)
    pl.semaphore_wait(barrier, len(peers))

    sent = []

    def send(src, dst, **peer):
        k = len(sent)
        copy = pltpu.make_async_remote_copy(
            src_ref=src, dst_ref=dst, send_sem=ssem.at[k], recv_sem=rsem.at[k],
            device_id=peer, device_id_type=MESH,
        )
        copy.start()
        sent.append(copy)
        return k, peer

    def arrive(handle, dst):
        k, peer = handle
        pltpu.make_async_remote_copy(
            src_ref=dst, dst_ref=dst, send_sem=ssem.at[k], recv_sem=rsem.at[k],
            device_id=peer, device_id_type=MESH,
        ).wait_recv()

    def column(k, lane):
        return 2 * ((y + k + 8) % 8) + lane

    def ring(buf, first):
        up, down = (y + 1) % 8, (y + 7) % 8
        to_partner = send(first, buf.at[t], tp=partner)
        right = {0: send(first, buf.at[t], tp=2 * up + l)}
        left = {0: send(first, buf.at[t], tp=2 * down + l)}
        yield
        arrive(to_partner, buf.at[partner])
        right[1] = send(buf.at[partner], buf.at[partner], tp=2 * up + l)
        left[1] = send(buf.at[partner], buf.at[partner], tp=2 * down + l)
        lanes = (l, other)
        for step in (1, 2):
            for q in range(2):
                yield
                a, b = buf.at[column(-step, lanes[q])], buf.at[column(step, lanes[q])]
                arrive(right[q], a)
                right[q] = send(a, a, tp=2 * up + l)
                arrive(left[q], b)
                left[q] = send(b, b, tp=2 * down + l)
        yield
        ends = []
        for q in range(2):
            arrive(right[q], buf.at[column(-3, lanes[q])])
            arrive(left[q], buf.at[column(3, lanes[q])])
        a, b = buf.at[column(-3, 0)], buf.at[column(3, 1)]
        ends.append((send(a, a, tp=2 * up + l), column(-4, 0)))
        ends.append((send(b, b, tp=2 * down + l), column(4, 1)))
        yield
        for handle, k in ends:
            arrive(handle, buf.at[k])

    local[2].wait()
    local[3].wait()
    features = ring(xb, xb.at[t])
    next(features)
    z_up = send(wb.at[g, s], wb.at[g, s], group=g_up)
    z_down = send(wb.at[g, s], wb.at[g, s], group=g_down)

    local[0].wait()
    local[1].wait()

    def text_part(which, j):
        part = tv[pl.ds(4 * j, 4), which].reshape(256, 512).astype(F32)
        part = jnp.minimum(jnp.maximum(part, -BIG), BIG)
        half = jnp.sum(part * part, axis=1, keepdims=True) * 0.5
        return dot((part * gain[...]).astype(BF16), kwv[...]), half

    @pl.loop(0, 2)
    def _(j):
        keys, half = text_part(other, j)
        tsend[pl.ds(4 * j, 4), :, :KV] = keys.astype(BF16).reshape(4, 64, KV)
        tsend[pl.ds(4 * j, 4), :, KV:] = three_parts(half).reshape(4, 64, PAD)

    @pl.loop(0, 2)
    def _(j):
        keys, half = text_part(l, j)
        lane = lax.broadcasted_iota(jnp.int32, (256, PAD), 1)
        town[pl.ds(4 * j, 4), :, :KV] = keys.reshape(4, 64, KV)
        town[pl.ds(4 * j, 4), :, KV:] = jnp.where(lane == 0, half, 0.0).reshape(4, 64, PAD)

    next(features)

    lo, hi = pl.ds(0, 128), pl.ds(128, 128)
    pieces = {}

    def spread(h):
        ref = wb.at[h, s]
        return [
            send(ref, ref, section=s_up), send(ref, ref, section=s_down),
            [(send(ref, ref, section=sib), wb.at[h, sib])],
        ]

    def spread_on(h, state):
        a, b = wb.at[h, s_down], wb.at[h, s_up]
        arrive(state[0], a)
        end_a = send(wb.at[h, s_down, lo], wb.at[h, s_down, lo], section=s_up)
        to_sib_a = send(a, a, section=sib)
        arrive(state[1], b)
        end_b = send(wb.at[h, s_up, hi], wb.at[h, s_up, hi], section=s_down)
        to_sib_b = send(b, b, section=sib)
        state[2] += [(to_sib_a, wb.at[h, (sib + 6) % 8]), (to_sib_b, wb.at[h, (sib + 2) % 8])]
        state[:2] = [end_a, end_b]

    def spread_last(h, state):
        arrive(state[0], wb.at[h, s_far, lo])
        arrive(state[1], wb.at[h, s_far, hi])
        ref = wb.at[h, s_far]
        state[2] += [(send(ref, ref, section=sib), wb.at[h, (sib + 4) % 8])]

    arrive(z_up, wb.at[g_down, s])
    far_up = send(wb.at[g_down, s, lo], wb.at[g_down, s, lo], group=g_up)
    pieces[0] = spread(g_down)
    arrive(z_down, wb.at[g_up, s])
    far_down = send(wb.at[g_up, s, hi], wb.at[g_up, s, hi], group=g_down)
    pieces[1] = spread(g_up)
    next(features)
    next(features)
    arrive(far_up, wb.at[g_far, s, lo])
    arrive(far_down, wb.at[g_far, s, hi])
    pieces[2] = spread(g_far)
    text_z = send(tsend, trecv, tp=partner)
    spread_on(g_down, pieces[0])
    spread_on(g_up, pieces[1])
    next(features)
    next(features)
    spread_on(g_far, pieces[2])
    next(features)
    spread_last(g_down, pieces[0])
    spread_last(g_up, pieces[1])
    spread_last(g_far, pieces[2])
    for _ in features:
        pass
    for k in range(3):
        for handle, ref in pieces[k][2]:
            arrive(handle, ref)

    acc[...] = jnp.zeros_like(acc)

    @pl.loop(0, 16)
    def _(k):
        acc[...] += dot(xb[k], wb[k // 4, pl.ds(2 * (k % 4), 2)].reshape(512, 512))

    image = (acc[...] + bias[...]).astype(BF16).astype(F32)
    half = jnp.sum(image * image, axis=1, keepdims=True) * 0.5
    isend[:, :, :KV] = dot((image * gain[...]).astype(BF16), kwv[...]).astype(BF16).reshape(16, 16, KV)
    isend[:, :, KV:] = three_parts(half).reshape(16, 16, PAD)
    parts = [
        send(isend.at[(t + d) % 16], irecv.at[d], tp=(t + d) % 16) for d in range(1, 16)
    ]

    arrive(text_z, trecv)

    @pl.loop(0, 8)
    def _(k):
        total = town[k] + trecv[k].astype(F32)
        town[k] = total
        ysend[k, :, :KV] = total[:, :KV].astype(BF16)
        ysend[k, :, KV:] = three_parts(jnp.sum(total[:, KV:], axis=1, keepdims=True))

    image = isend[t].astype(F32)
    for d in range(1, 16):
        arrive(parts[d - 1], irecv.at[d])
        image += irecv[d].astype(F32)
    scale = inverse_rms(jnp.sum(image[:, KV:], axis=1, keepdims=True))
    ikey[...] = (image[:, :KV] * scale).astype(BF16)
    placed = [send(ikey, dest.at[g], section=s_far, group=(g + d) % 4) for d in range(4)]
    windows = [
        send(ysend.at[(y + d) % 8], yrecv.at[d], tp=2 * ((y + d) % 8) + l) for d in range(1, 8)
    ]

    taken = jnp.int32(0)
    starts = [jnp.int32(1 << 20), jnp.int32(1 << 20)]
    picks = []
    for k in range(4):
        mine = grp[s_far * 4 + k] == g
        start = off[s_far * 4 + k]
        slot = jnp.where(mine, taken, 2)
        picks.append(slot)
        starts = [jnp.where(slot == a, start, starts[a]) for a in range(2)]
        taken = taken + jnp.where(mine, 1, 0)
    for k in range(4):
        arrive(placed[k], dest.at[(g + 4 - k) % 4])
    for a in range(2):
        chosen = jnp.zeros((16, KV), F32)
        for k in range(4):
            chosen = jnp.where(picks[k] == a, dest[k].astype(F32), chosen)
        ag[t, a] = chosen.astype(BF16)
    for _ in ring(ag, ag.at[t]):
        pass

    text = town[y]
    for d in range(1, 8):
        arrive(windows[d - 1], yrecv.at[d])
        text += yrecv[d].astype(F32)
    keys = text[:, :KV] * inverse_rms(jnp.sum(text[:, KV:], axis=1, keepdims=True))
    rows = lax.broadcasted_iota(jnp.int32, (64, 256), 0) + 64 * t
    columns = lax.broadcasted_iota(jnp.int32, (64, 256), 1)
    row = lax.broadcasted_iota(jnp.int32, (64, 1), 0) + 64 * t
    for a in range(2):
        hit = jnp.where(rows - starts[a] == columns, 1.0, 0.0).astype(BF16)
        image = dot(hit, ag[:, a].reshape(256, KV))
        inside = (row >= starts[a]) & (row < starts[a] + 256)
        keys = jnp.where(inside, image, keys)
    out[...] = keys.astype(BF16)

    for copy in sent:
        copy.wait_send()


def on_device(vis, wp, bias, txt, gain, kw, grp, off):
    any_space = pl.BlockSpec(memory_space=pl.ANY)
    vmem = pl.BlockSpec(memory_space=pltpu.VMEM)
    smem = pl.BlockSpec(memory_space=pltpu.SMEM)
    return pl.pallas_call(
        kernel,
        out_shape=jax.ShapeDtypeStruct((64, KV), BF16),
        in_specs=[any_space, any_space, vmem, any_space, vmem, any_space, smem, smem],
        out_specs=vmem,
        scratch_shapes=[
            pltpu.VMEM((16, 256, 512), BF16),
            pltpu.VMEM((4, 8, 256, 512), BF16),
            pltpu.VMEM((8, 2, 64, 512), BF16),
            pltpu.VMEM((512, KV), BF16),
            pltpu.VMEM((8, 64, WIDE), BF16),
            pltpu.VMEM((8, 64, WIDE), BF16),
            pltpu.VMEM((8, 64, WIDE), F32),
            pltpu.VMEM((8, 64, WIDE), BF16),
            pltpu.VMEM((8, 64, WIDE), BF16),
            pltpu.VMEM((256, 512), F32),
            pltpu.VMEM((16, 16, WIDE), BF16),
            pltpu.VMEM((16, 16, WIDE), BF16),
            pltpu.VMEM((16, KV), BF16),
            pltpu.VMEM((4, 16, KV), BF16),
            pltpu.VMEM((16, 2, 16, KV), BF16),
            pltpu.SemaphoreType.DMA((SEMS,)),
            pltpu.SemaphoreType.DMA((SEMS,)),
            pltpu.SemaphoreType.DMA((4,)),
        ],
        compiler_params=pltpu.CompilerParams(
            collective_id=0, has_side_effects=True, vmem_limit_bytes=48 * 1024 * 1024
        ),
    )(
        vis,
        wp.reshape(8, 256, 512),
        bias.astype(F32).reshape(1, 512),
        txt.reshape(8, 2, 64, 512),
        gain.reshape(1, 512),
        kw,
        grp,
        off,
    )


def solution(mesh):
    in_specs = (
        P(("section", "group"), "tp"),
        P("group", "tp"),
        P("tp"),
        P(("section", "group"), "tp"),
        P("tp"),
        P("tp", None),
        P(),
        P(),
    )
    out_specs = P(("section", "group", "tp"), None)
    return jax.shard_map(
        on_device, mesh=mesh, in_specs=in_specs, out_specs=out_specs, check_vma=False
    )
```

```python
import jax
import jax.numpy as jnp
from jax import lax
from jax.experimental import pallas as pl
from jax.experimental.pallas import tpu as pltpu
from jax.sharding import PartitionSpec as P

MESH = pl.DeviceIdType.MESH
D = 8192
KV = 1024
PAD = 128
WIDE = KV + PAD
EPS = 1e-05
BIG = 1.9e19
F32 = jnp.float32
BF16 = jnp.bfloat16
SEMS = 128
VMEM_BYTES = 62 * 1024 * 1024


def dot(a, b):
    return jnp.dot(a, b, preferred_element_type=F32)


def three_parts(v):
    lane = lax.broadcasted_iota(jnp.int32, (v.shape[0], PAD), 1)
    hi = v.astype(BF16).astype(F32)
    rest = jnp.where(hi < jnp.inf, v - hi, 0.0)
    mid = rest.astype(BF16).astype(F32)
    low = rest - mid
    parts = jnp.where(lane == 0, hi, jnp.where(lane == 1, mid, jnp.where(lane == 2, low, 0.0)))
    return parts.astype(BF16)


def inverse_rms(half_sum):
    return 1.0 / jnp.sqrt(half_sum * 2.0 / D + EPS)


def kernel(
    vis, wp, bias_in, txt, gain_in, kw, grp_in, off_in, out,
    bias, gain, grp, off, xb, wb, tv, kwv, tsend, trecv, town, csend, crecv, acc, isend, irecv,
    ikey, dest, asend, fin, ssem, rsem, lsem,
):
    s, g, t = lax.axis_index("section"), lax.axis_index("group"), lax.axis_index("tp")
    y, l = t // 2, t % 2
    other = 1 - l
    partner = 2 * y + other
    up, down = 2 * ((y + 1) % 8) + l, 2 * ((y + 7) % 8) + l
    sib = s + 1 - 2 * (s % 2)
    g_up, g_down, g_far = (g + 1) % 4, (g + 3) % 4, (g + 2) % 4
    s_up, s_down, s_far = (s + 2) % 8, (s + 6) % 8, (s + 4) % 8

    local = []
    pairs = (
        (txt, tv), (kw, kwv), (gain_in, gain), (vis, xb.at[t]), (wp, wb.at[pl.ds(8 * g, 8)]),
        (bias_in, bias), (grp_in, grp), (off_in, off),
    )
    for k, (src, dst) in enumerate(pairs):
        copy = pltpu.make_async_copy(src, dst, lsem.at[k])
        copy.start()
        local.append(copy)

    peers = [{"tp": partner}, {"tp": up}, {"tp": down}, {"group": g_up}, {"group": g_down}]
    peers += [{"section": s_up}, {"section": s_down}, {"section": sib}]
    barrier = pltpu.get_barrier_semaphore()
    for peer in peers:
        pl.semaphore_signal(barrier, inc=1, device_id=peer, device_id_type=MESH)
    pl.semaphore_wait(barrier, len(peers))

    sent = []

    def send(src, dst, **peer):
        k = len(sent)
        copy = pltpu.make_async_remote_copy(
            src_ref=src, dst_ref=dst, send_sem=ssem.at[k], recv_sem=rsem.at[k],
            device_id=peer, device_id_type=MESH,
        )
        copy.start()
        sent.append(copy)
        return k, peer

    def pass_on(ref, **peer):
        return send(ref, ref, **peer)

    def arrive(handle, dst):
        k, peer = handle
        pltpu.make_async_remote_copy(
            src_ref=dst, dst_ref=dst, send_sem=ssem.at[k], recv_sem=rsem.at[k],
            device_id=peer, device_id_type=MESH,
        ).wait_recv()

    lo, hi = pl.ds(0, 128), pl.ds(128, 128)

    def block(k, lane):
        return xb.at[2 * ((y + k + 8) % 8) + lane]

    lanes = (l, other)
    right, left = {}, {}

    def ring_start():
        right[0] = send(vis, xb.at[t], tp=up)
        left[0] = send(vis, xb.at[t], tp=down)

    def ring_partner():
        arrive(to_partner, xb.at[partner])
        right[1] = pass_on(xb.at[partner], tp=up)
        left[1] = pass_on(xb.at[partner], tp=down)

    def ring_on(q, step):
        a, b = block(-step, lanes[q]), block(step, lanes[q])
        arrive(right[q], a)
        if step < 3:
            right[q] = pass_on(a, tp=up)
        else:
            right[q] = pass_on(a.at[lo], tp=up)
        arrive(left[q], b)
        if step < 3:
            left[q] = pass_on(b, tp=down)
        else:
            left[q] = pass_on(b.at[hi], tp=down)

    def ring_end(q):
        arrive(right[q], block(4, lanes[q]).at[lo])
        arrive(left[q], block(4, lanes[q]).at[hi])

    groups = {"down": g_down, "up": g_up, "far": g_far}

    def piece(h, section):
        return wb.at[8 * (groups[h] if isinstance(h, str) else h) + section]

    along, to_sib = {}, []

    def spread(h, rows, name):
        ref = piece(h, s).at[rows]
        along[name, h] = (pass_on(ref, section=s_up), pass_on(ref, section=s_down))

    def to_core(h, section, rows=pl.ds(0, 256)):
        handle = pass_on(piece(h, section).at[rows], section=sib)
        to_sib.append((handle, piece(h, (section + sib - s + 8) % 8).at[rows]))

    def spread_on(h):
        arrive(along["lo", h][0], piece(h, s_down).at[lo])
        end_lo = pass_on(piece(h, s_down).at[lo], section=s_up)
        arrive(along["hi", h][1], piece(h, s_up).at[hi])
        end_hi = pass_on(piece(h, s_up).at[hi], section=s_down)
        arrive(along["hi", h][0], piece(h, s_down).at[hi])
        to_core(h, s_down)
        arrive(along["lo", h][1], piece(h, s_up).at[lo])
        to_core(h, s_up)
        along["end", h] = (end_lo, end_hi)

    def spread_end(h):
        arrive(along["end", h][0], piece(h, s_far).at[lo])
        to_core(h, s_far, lo)
        arrive(along["end", h][1], piece(h, s_far).at[hi])
        to_core(h, s_far, hi)

    to_partner = send(vis, xb.at[t], tp=partner)
    ring_start()
    z_up, z_down = {}, {}
    for rows, first in ((lo, 0), (hi, 128)):
        z_up[first] = send(wp.at[s, rows], piece(g, s).at[rows], group=g_up)
        flip = hi if first == 0 else lo
        z_down[128 - first] = send(wp.at[s, flip], piece(g, s).at[flip], group=g_down)

    for k in range(3):
        local[k].wait()

    def text_part(which, j):
        part = tv[pl.ds(4 * j, 4), which].reshape(256, 512).astype(F32)
        part = jnp.minimum(jnp.maximum(part, -BIG), BIG)
        half = jnp.sum(part * part, axis=1, keepdims=True) * 0.5
        part = part * gain[...]
        coarse = part.astype(BF16)
        fine = (part - coarse.astype(F32)).astype(BF16)
        return dot(coarse, kwv[...]) + dot(fine, kwv[...]), half

    @pl.loop(0, 2)
    def _(j):
        keys, half = text_part(other, j)
        tsend[pl.ds(4 * j, 4), :, :KV] = keys.astype(BF16).reshape(4, 64, KV)
        tsend[pl.ds(4 * j, 4), :, KV:] = three_parts(half).reshape(4, 64, PAD)

    ring_on(0, 1)

    @pl.loop(0, 2)
    def _(j):
        keys, half = text_part(l, j)
        lane = lax.broadcasted_iota(jnp.int32, (256, PAD), 1)
        town[pl.ds(4 * j, 4), :, :KV] = keys.reshape(4, 64, KV)
        town[pl.ds(4 * j, 4), :, KV:] = jnp.where(lane == 0, half, 0.0).reshape(4, 64, PAD)

    arrive(z_up[0], piece("down", s).at[lo])
    far_lo = pass_on(piece("down", s).at[lo], group=g_up)
    spread("down", lo, "lo")
    arrive(z_down[128], piece("up", s).at[hi])
    far_hi = pass_on(piece("up", s).at[hi], group=g_down)
    spread("up", hi, "hi")
    ring_partner()
    arrive(z_up[128], piece("down", s).at[hi])
    spread("down", hi, "hi")
    to_core("down", s)
    arrive(z_down[0], piece("up", s).at[lo])
    spread("up", lo, "lo")
    to_core("up", s)
    ring_on(0, 2)
    arrive(far_lo, piece("far", s).at[lo])
    spread("far", lo, "lo")
    arrive(far_hi, piece("far", s).at[hi])
    spread("far", hi, "hi")
    to_core("far", s)
    text_z = send(tsend, trecv, tp=partner)
    ring_on(1, 1)
    spread_on("down")
    spread_on("up")
    ring_on(0, 3)
    ring_on(1, 2)
    spread_on("far")
    spread_end("down")
    spread_end("up")
    ring_on(1, 3)
    spread_end("far")
    for k in range(3, 8):
        local[k].wait()
    for handle, ref in to_sib:
        arrive(handle, ref)

    def project(k):
        w = wb[pl.ds(4 * k, 4)].reshape(1024, 512)
        return dot(xb[2 * k], w[:512]) + dot(xb[2 * k + 1], w[512:])

    acc[...] = jnp.zeros_like(acc) + bias[...].astype(F32)

    @pl.loop(0, 7)
    def _(k):
        acc[...] += project((y + 5 + k) % 8)

    ring_end(0)
    ring_end(1)
    image = (acc[...] + project((y + 4) % 8)).astype(BF16)

    own_start = off[4 * s + g]
    turned = (lax.broadcasted_iota(jnp.int32, (256, 256), 0) - own_start) & 255
    turn = jnp.where(turned == lax.broadcasted_iota(jnp.int32, (256, 256), 1), 1.0, 0.0)
    image = dot(turn.astype(BF16), image)
    half = jnp.sum(image * image, axis=1, keepdims=True) * 0.5
    isend[:, :, KV:] = three_parts(half).reshape(16, 16, PAD)
    isend[:, :, :KV] = dot((image * gain[...]).astype(BF16), kwv[...]).astype(BF16).reshape(16, 16, KV)
    parts = [
        send(isend.at[(t + d) % 16], irecv.at[d], tp=(t + d) % 16) for d in range(1, 16)
    ]

    arrive(text_z, trecv)

    @pl.loop(0, 8)
    def _(k):
        town[k] += trecv[k].astype(F32)

    chain = {}

    def chain_on(step):
        for way, (to, sign) in enumerate(((up, 1), (down, 7))):
            rows = pl.ds(0, 64)
            if step == 1:
                rows = pl.ds(32 * way, 32)
            total = town[(y + sign * (5 - step)) % 8, rows]
            if step == 2:
                first = pl.ds(32 * way, 32)
                arrive(chain[way], crecv.at[way, 0, first])
                came = crecv[way, 0, first].astype(F32)
                empty = jnp.zeros_like(came)
                total += jnp.concatenate([came, empty] if way == 0 else [empty, came], axis=0)
            elif step > 2:
                arrive(chain[way], crecv.at[way, step - 2])
                total += crecv[way, step - 2].astype(F32)
            csend[way, step - 1, rows, :KV] = total[:, :KV].astype(BF16)
            csend[way, step - 1, rows, KV:] = three_parts(
                jnp.sum(total[:, KV:], axis=1, keepdims=True)
            )
            chain[way] = send(
                csend.at[way, step - 1, rows], crecv.at[way, step - 1, rows], tp=to
            )

    chain_on(1)
    image = isend[t].astype(F32)
    for d in range(1, 16):
        arrive(parts[d - 1], irecv.at[d])
        image += irecv[d].astype(F32)
    scale = inverse_rms(jnp.sum(image[:, KV:], axis=1, keepdims=True))
    ikey[...] = (image[:, :KV] * scale).astype(BF16)
    placed = [send(ikey, dest.at[g], section=s_far, group=(g + d) % 4) for d in range(4)]
    chain_on(2)

    starts = [
        jnp.where(grp[s_far * 4 + k] == g, off[s_far * 4 + k], 1 << 20) for k in range(4)
    ]

    def inside(row, k):
        return (row >= starts[k]) & (row < starts[k] + 256)

    for k in range(4):
        arrive(placed[k], dest.at[(g + 4 - k) % 4])
    base = SEMS - 4
    slot = t % 4
    last = []
    for m in range(4):
        row = lax.broadcasted_iota(jnp.int32, (16, 1), 0) + 256 * m + 16 * t
        chosen = jnp.zeros((16, KV), F32)
        for k in range(4):
            chosen = jnp.where(inside(row, k), dest[k].astype(F32), chosen)
        asend[m] = chosen.astype(BF16)
        target = t // 4 + 4 * m
        copy = pltpu.make_async_remote_copy(
            src_ref=asend.at[m], dst_ref=fin.at[slot], send_sem=ssem.at[base + m],
            recv_sem=rsem.at[base + slot], device_id={"tp": target}, device_id_type=MESH,
        )
        last.append((copy, target))

        @pl.when(target != t)
        def _():
            copy.start()

        @pl.when(target == t)
        def _():
            fin[slot] = asend[m]

    chain_on(3)
    chain_on(4)
    text = town[y]
    for way in range(2):
        arrive(chain[way], crecv.at[way, 3])
        text += crecv[way, 3].astype(F32)
    keys = text[:, :KV] * inverse_rms(jnp.sum(text[:, KV:], axis=1, keepdims=True))
    for j in range(4):
        source = 4 * (t % 4) + j

        @pl.when(source != t)
        def _():
            pltpu.make_async_remote_copy(
                src_ref=fin.at[j], dst_ref=fin.at[j], send_sem=ssem.at[base + j],
                recv_sem=rsem.at[base + j], device_id={"tp": source}, device_id_type=MESH,
            ).wait_recv()

    row = lax.broadcasted_iota(jnp.int32, (64, 1), 0) + 64 * t
    hit = inside(row, 0) | inside(row, 1) | inside(row, 2) | inside(row, 3)
    out[...] = jnp.where(hit, fin[...].reshape(64, KV).astype(F32), keys).astype(BF16)

    for copy in sent:
        copy.wait_send()
    for copy, target in last:

        @pl.when(target != t)
        def _():
            copy.wait_send()


def on_device(vis, wp, bias, txt, gain, kw, grp, off):
    return pl.pallas_call(
        kernel,
        out_shape=jax.ShapeDtypeStruct((64, KV), BF16),
        in_specs=[pl.BlockSpec(memory_space=pl.ANY)] * 8,
        out_specs=pl.BlockSpec(memory_space=pltpu.VMEM),
        scratch_shapes=[
            pltpu.VMEM((1, 512), BF16),
            pltpu.VMEM((1, 512), F32),
            pltpu.SMEM((32,), jnp.int32),
            pltpu.SMEM((32,), jnp.int32),
            pltpu.VMEM((16, 256, 512), BF16),
            pltpu.VMEM((32, 256, 512), BF16),
            pltpu.VMEM((8, 2, 64, 512), BF16),
            pltpu.VMEM((512, KV), BF16),
            pltpu.VMEM((8, 64, WIDE), BF16),
            pltpu.VMEM((8, 64, WIDE), BF16),
            pltpu.VMEM((8, 64, WIDE), F32),
            pltpu.VMEM((2, 4, 64, WIDE), BF16),
            pltpu.VMEM((2, 4, 64, WIDE), BF16),
            pltpu.VMEM((256, 512), F32),
            pltpu.VMEM((16, 16, WIDE), BF16),
            pltpu.VMEM((16, 16, WIDE), BF16),
            pltpu.VMEM((16, KV), BF16),
            pltpu.VMEM((4, 16, KV), BF16),
            pltpu.VMEM((4, 16, KV), BF16),
            pltpu.VMEM((4, 16, KV), BF16),
            pltpu.SemaphoreType.DMA((SEMS,)),
            pltpu.SemaphoreType.DMA((SEMS,)),
            pltpu.SemaphoreType.DMA((8,)),
        ],
        compiler_params=pltpu.CompilerParams(
            collective_id=0, has_side_effects=True, vmem_limit_bytes=VMEM_BYTES
        ),
    )(
        vis,
        wp.reshape(8, 256, 512),
        bias.reshape(1, 512),
        txt.reshape(8, 2, 64, 512),
        gain.reshape(1, 512),
        kw,
        grp,
        off,
    )


def solution(mesh):
    in_specs = (
        P(("section", "group"), "tp"),
        P("group", "tp"),
        P("tp"),
        P(("section", "group"), "tp"),
        P("tp"),
        P("tp", None),
        P(),
        P(),
    )
    out_specs = P(("section", "group", "tp"), None)
    return jax.shard_map(
        on_device, mesh=mesh, in_specs=in_specs, out_specs=out_specs, check_vma=False
    )
```

```python
import jax
import jax.numpy as jnp
from jax import lax
from jax.experimental import pallas as pl
from jax.experimental.pallas import tpu as pltpu
from jax.sharding import PartitionSpec as P

MESH = pl.DeviceIdType.MESH
D = 8192
KV = 1024
PAD = 128
WIDE = KV + PAD
EPS = 1e-05
BIG = 1.9e19
F32 = jnp.float32
BF16 = jnp.bfloat16
SEMS = 128
VMEM_BYTES = 62 * 1024 * 1024


def dot(a, b):
    return jnp.dot(a, b, preferred_element_type=F32)


def three_parts(v):
    lane = lax.broadcasted_iota(jnp.int32, (v.shape[0], PAD), 1)
    hi = v.astype(BF16).astype(F32)
    rest = jnp.where(hi < jnp.inf, v - hi, 0.0)
    mid = rest.astype(BF16).astype(F32)
    low = rest - mid
    parts = jnp.where(lane == 0, hi, jnp.where(lane == 1, mid, jnp.where(lane == 2, low, 0.0)))
    return parts.astype(BF16)


def inverse_rms(half_sum):
    return 1.0 / jnp.sqrt(half_sum * 2.0 / D + EPS)


def kernel(
    vis, wp, bias_in, txt, gain_in, kw, grp_in, off_in, out,
    bias, gain, grp, off, xb, wb, tv, kwv, tsend, trecv, town, csend, crecv, acc, isend, irecv,
    ikey, dest, asend, fin, ssem, rsem, lsem,
):
    s, g, t = lax.axis_index("section"), lax.axis_index("group"), lax.axis_index("tp")
    y, l = t // 2, t % 2
    other = 1 - l
    partner = 2 * y + other
    up, down = 2 * ((y + 1) % 8) + l, 2 * ((y + 7) % 8) + l
    sib = s + 1 - 2 * (s % 2)
    g_up, g_down, g_far = (g + 1) % 4, (g + 3) % 4, (g + 2) % 4
    s_up, s_down, s_far = (s + 2) % 8, (s + 6) % 8, (s + 4) % 8

    local = []
    pairs = (
        (txt, tv), (kw, kwv), (gain_in, gain), (vis, xb.at[t]), (wp, wb.at[pl.ds(8 * g, 8)]),
        (bias_in, bias), (grp_in, grp), (off_in, off),
    )
    for k, (src, dst) in enumerate(pairs):
        copy = pltpu.make_async_copy(src, dst, lsem.at[k])
        copy.start()
        local.append(copy)

    peers = [{"tp": partner}, {"tp": up}, {"tp": down}, {"group": g_up}, {"group": g_down}]
    peers += [{"section": s_up}, {"section": s_down}, {"section": sib}]
    barrier = pltpu.get_barrier_semaphore()
    for peer in peers:
        pl.semaphore_signal(barrier, inc=1, device_id=peer, device_id_type=MESH)
    pl.semaphore_wait(barrier, len(peers))

    sent = []

    def send(src, dst, **peer):
        k = len(sent)
        copy = pltpu.make_async_remote_copy(
            src_ref=src, dst_ref=dst, send_sem=ssem.at[k], recv_sem=rsem.at[k],
            device_id=peer, device_id_type=MESH,
        )
        copy.start()
        sent.append(copy)
        return k, peer

    def pass_on(ref, **peer):
        return send(ref, ref, **peer)

    def arrive(handle, dst):
        k, peer = handle
        pltpu.make_async_remote_copy(
            src_ref=dst, dst_ref=dst, send_sem=ssem.at[k], recv_sem=rsem.at[k],
            device_id=peer, device_id_type=MESH,
        ).wait_recv()

    lo, hi = pl.ds(0, 128), pl.ds(128, 128)

    def block(k, lane):
        return xb.at[2 * ((y + k + 8) % 8) + lane]

    lanes = (l, other)
    halves = (lo, hi)
    right, left = {}, {}

    def ring_start(q, half):
        ref = xb.at[t, halves[half]]
        if q == 0:
            src = vis.at[halves[half]]
        else:
            arrive(to_partner[half], xb.at[partner, halves[half]])
            src = ref = xb.at[partner, halves[half]]
        right[q, half] = send(src, ref, tp=up)
        left[q, half] = send(src, ref, tp=down)

    def ring_on(q, half, step):
        a, b = block(-step, lanes[q]).at[halves[half]], block(step, lanes[q]).at[halves[half]]
        arrive(right[q, half], a)
        if step < 3 or half == 0:
            right[q, half] = pass_on(a, tp=up)
        arrive(left[q, half], b)
        if step < 3 or half == 1:
            left[q, half] = pass_on(b, tp=down)

    def ring_end(q):
        arrive(right[q, 0], block(4, lanes[q]).at[lo])
        arrive(left[q, 1], block(4, lanes[q]).at[hi])

    groups = {"down": g_down, "up": g_up, "far": g_far}

    def piece(h, section):
        return wb.at[8 * (groups[h] if isinstance(h, str) else h) + section]

    along, to_sib = {}, []

    def spread(h, rows, name):
        ref = piece(h, s).at[rows]
        along[name, h] = (pass_on(ref, section=s_up), pass_on(ref, section=s_down))

    def to_core(h, section, rows=pl.ds(0, 256)):
        handle = pass_on(piece(h, section).at[rows], section=sib)
        to_sib.append((handle, piece(h, (section + sib - s + 8) % 8).at[rows]))

    def spread_on(h):
        arrive(along["lo", h][0], piece(h, s_down).at[lo])
        end_lo = pass_on(piece(h, s_down).at[lo], section=s_up)
        arrive(along["hi", h][1], piece(h, s_up).at[hi])
        end_hi = pass_on(piece(h, s_up).at[hi], section=s_down)
        arrive(along["hi", h][0], piece(h, s_down).at[hi])
        to_core(h, s_down)
        arrive(along["lo", h][1], piece(h, s_up).at[lo])
        to_core(h, s_up)
        along["end", h] = (end_lo, end_hi)

    def spread_end(h):
        arrive(along["end", h][0], piece(h, s_far).at[lo])
        to_core(h, s_far, lo)
        arrive(along["end", h][1], piece(h, s_far).at[hi])
        to_core(h, s_far, hi)

    to_partner = [send(vis.at[half], xb.at[t, half], tp=partner) for half in halves]
    ring_start(0, 0)
    ring_start(0, 1)
    z_up, z_down = {}, {}
    for rows, first in ((lo, 0), (hi, 128)):
        z_up[first] = send(wp.at[s, rows], piece(g, s).at[rows], group=g_up)
        flip = hi if first == 0 else lo
        z_down[128 - first] = send(wp.at[s, flip], piece(g, s).at[flip], group=g_down)

    for k in range(3):
        local[k].wait()

    def text_part(which, j):
        part = tv[pl.ds(4 * j, 4), which].reshape(256, 512).astype(F32)
        part = jnp.minimum(jnp.maximum(part, -BIG), BIG)
        half = jnp.sum(part * part, axis=1, keepdims=True) * 0.5
        part = part * gain[...]
        coarse = part.astype(BF16)
        fine = (part - coarse.astype(F32)).astype(BF16)
        return dot(coarse, kwv[...]) + dot(fine, kwv[...]), half

    def text_for_partner(j):
        keys, half = text_part(other, j)
        tsend[pl.ds(4 * j, 4), :, :KV] = keys.astype(BF16).reshape(4, 64, KV)
        tsend[pl.ds(4 * j, 4), :, KV:] = three_parts(half).reshape(4, 64, PAD)

    def text_here(j):
        keys, half = text_part(l, j)
        lane = lax.broadcasted_iota(jnp.int32, (256, PAD), 1)
        town[pl.ds(4 * j, 4), :, :KV] = keys.reshape(4, 64, KV)
        town[pl.ds(4 * j, 4), :, KV:] = jnp.where(lane == 0, half, 0.0).reshape(4, 64, PAD)

    text_for_partner(0)
    ring_on(0, 0, 1)
    text_for_partner(1)
    ring_on(0, 1, 1)
    ring_start(1, 0)
    arrive(z_up[0], piece("down", s).at[lo])
    far_lo = pass_on(piece("down", s).at[lo], group=g_up)
    spread("down", lo, "lo")
    arrive(z_down[128], piece("up", s).at[hi])
    far_hi = pass_on(piece("up", s).at[hi], group=g_down)
    spread("up", hi, "hi")
    ring_start(1, 1)
    ring_on(0, 0, 2)
    text_here(0)
    arrive(z_up[128], piece("down", s).at[hi])
    spread("down", hi, "hi")
    to_core("down", s)
    arrive(z_down[0], piece("up", s).at[lo])
    spread("up", lo, "lo")
    to_core("up", s)
    ring_on(1, 0, 1)
    text_here(1)
    ring_on(1, 1, 1)
    ring_on(0, 1, 2)
    arrive(far_lo, piece("far", s).at[lo])
    spread("far", lo, "lo")
    arrive(far_hi, piece("far", s).at[hi])
    spread("far", hi, "hi")
    to_core("far", s)
    text_z = {}
    for k in (4, 5, 3, 6, 2, 7, 1, 0):
        window = (y + k) % 8
        text_z[k] = send(tsend.at[window], trecv.at[window], tp=partner)
    spread_on("down")
    ring_on(1, 0, 2)
    spread_on("up")
    ring_on(1, 1, 2)
    ring_on(0, 0, 3)
    ring_on(0, 1, 3)
    spread_on("far")
    ring_on(1, 0, 3)
    spread_end("down")
    spread_end("up")
    ring_on(1, 1, 3)
    spread_end("far")
    for k in range(3, 8):
        local[k].wait()
    for handle, ref in to_sib:
        arrive(handle, ref)

    chain = {}

    def chain_on(step):
        for way, (to, sign) in enumerate(((up, 1), (down, 7))):
            rows = pl.ds(0, 64)
            if step == 1:
                rows = pl.ds(32 * way, 32)
            k = sign * (5 - step) % 8
            window = (y + k) % 8
            if step > 1 or way == 0:
                arrive(text_z[k], trecv.at[window])
            total = town[window, rows] + trecv[window, rows].astype(F32)
            if step == 2:
                first = pl.ds(32 * way, 32)
                arrive(chain[way], crecv.at[way, 0, first])
                came = crecv[way, 0, first].astype(F32)
                empty = jnp.zeros_like(came)
                total += jnp.concatenate([came, empty] if way == 0 else [empty, came], axis=0)
            elif step > 2:
                arrive(chain[way], crecv.at[way, step - 2])
                total += crecv[way, step - 2].astype(F32)
            csend[way, step - 1, rows, :KV] = total[:, :KV].astype(BF16)
            csend[way, step - 1, rows, KV:] = three_parts(
                jnp.sum(total[:, KV:], axis=1, keepdims=True)
            )
            chain[way] = send(
                csend.at[way, step - 1, rows], crecv.at[way, step - 1, rows], tp=to
            )

    def project(k):
        w = wb[pl.ds(4 * k, 4)].reshape(1024, 512)
        return dot(xb[2 * k], w[:512]) + dot(xb[2 * k + 1], w[512:])

    acc[...] = jnp.zeros_like(acc) + bias[...].astype(F32).reshape(1, 512)

    @pl.loop(0, 7)
    def _(k):
        acc[...] += project((y + 5 + k) % 8)

    chain_on(1)
    ring_end(0)
    ring_end(1)
    image = (acc[...] + project((y + 4) % 8)).astype(BF16)

    own_start = off[4 * s + g]
    turned = (lax.broadcasted_iota(jnp.int32, (256, 256), 0) - own_start) & 255
    turn = jnp.where(turned == lax.broadcasted_iota(jnp.int32, (256, 256), 1), 1.0, 0.0)
    image = dot(turn.astype(BF16), image)
    half = jnp.sum(image * image, axis=1, keepdims=True) * 0.5
    isend[:, :, KV:] = three_parts(half).reshape(16, 16, PAD)
    isend[:, :, :KV] = dot((image * gain[...]).astype(BF16), kwv[...]).astype(BF16).reshape(16, 16, KV)
    parts = [
        send(isend.at[(t + d) % 16], irecv.at[d], tp=(t + d) % 16) for d in range(1, 16)
    ]

    chain_on(2)
    image = isend[t].astype(F32)
    for d in range(1, 16):
        arrive(parts[d - 1], irecv.at[d])
        image += irecv[d].astype(F32)
    scale = inverse_rms(jnp.sum(image[:, KV:], axis=1, keepdims=True))
    ikey[...] = (image[:, :KV] * scale).astype(BF16)
    placed = [send(ikey, dest.at[g], section=s_far, group=(g + d) % 4) for d in range(4)]
    chain_on(3)

    starts = [
        jnp.where(grp[s_far * 4 + k] == g, off[s_far * 4 + k], 1 << 20) for k in range(4)
    ]

    def inside(row, k):
        return (row >= starts[k]) & (row < starts[k] + 256)

    for k in range(4):
        arrive(placed[k], dest.at[(g + 4 - k) % 4])
    base = SEMS - 4
    slot = t % 4
    last = []
    for m in range(4):
        row = lax.broadcasted_iota(jnp.int32, (16, 1), 0) + 256 * m + 16 * t
        chosen = jnp.zeros((16, KV), F32)
        for k in range(4):
            chosen = jnp.where(inside(row, k), dest[k].astype(F32), chosen)
        asend[m] = chosen.astype(BF16)
        target = t // 4 + 4 * m
        copy = pltpu.make_async_remote_copy(
            src_ref=asend.at[m], dst_ref=fin.at[slot], send_sem=ssem.at[base + m],
            recv_sem=rsem.at[base + slot], device_id={"tp": target}, device_id_type=MESH,
        )
        last.append((copy, target))

        @pl.when(target != t)
        def _():
            copy.start()

        @pl.when(target == t)
        def _():
            fin[slot] = asend[m]

    chain_on(4)
    arrive(text_z[0], trecv.at[y])
    text = town[y] + trecv[y].astype(F32)
    for way in range(2):
        arrive(chain[way], crecv.at[way, 3])
        text += crecv[way, 3].astype(F32)
    keys = text[:, :KV] * inverse_rms(jnp.sum(text[:, KV:], axis=1, keepdims=True))
    for j in range(4):
        source = 4 * (t % 4) + j

        @pl.when(source != t)
        def _():
            pltpu.make_async_remote_copy(
                src_ref=fin.at[j], dst_ref=fin.at[j], send_sem=ssem.at[base + j],
                recv_sem=rsem.at[base + j], device_id={"tp": source}, device_id_type=MESH,
            ).wait_recv()

    row = lax.broadcasted_iota(jnp.int32, (64, 1), 0) + 64 * t
    hit = inside(row, 0) | inside(row, 1) | inside(row, 2) | inside(row, 3)
    out[...] = jnp.where(hit, fin[...].reshape(64, KV).astype(F32), keys).astype(BF16)

    for copy in sent:
        copy.wait_send()
    for copy, target in last:

        @pl.when(target != t)
        def _():
            copy.wait_send()


def on_device(vis, wp, bias, txt, gain, kw, grp, off):
    return pl.pallas_call(
        kernel,
        out_shape=jax.ShapeDtypeStruct((64, KV), BF16),
        in_specs=[pl.BlockSpec(memory_space=pl.ANY)] * 8,
        out_specs=pl.BlockSpec(memory_space=pltpu.VMEM),
        scratch_shapes=[
            pltpu.VMEM((512,), BF16),
            pltpu.VMEM((1, 512), F32),
            pltpu.SMEM((32,), jnp.int32),
            pltpu.SMEM((32,), jnp.int32),
            pltpu.VMEM((16, 256, 512), BF16),
            pltpu.VMEM((32, 256, 512), BF16),
            pltpu.VMEM((8, 2, 64, 512), BF16),
            pltpu.VMEM((512, KV), BF16),
            pltpu.VMEM((8, 64, WIDE), BF16),
            pltpu.VMEM((8, 64, WIDE), BF16),
            pltpu.VMEM((8, 64, WIDE), F32),
            pltpu.VMEM((2, 4, 64, WIDE), BF16),
            pltpu.VMEM((2, 4, 64, WIDE), BF16),
            pltpu.VMEM((256, 512), F32),
            pltpu.VMEM((16, 16, WIDE), BF16),
            pltpu.VMEM((16, 16, WIDE), BF16),
            pltpu.VMEM((16, KV), BF16),
            pltpu.VMEM((4, 16, KV), BF16),
            pltpu.VMEM((4, 16, KV), BF16),
            pltpu.VMEM((4, 16, KV), BF16),
            pltpu.SemaphoreType.DMA((SEMS,)),
            pltpu.SemaphoreType.DMA((SEMS,)),
            pltpu.SemaphoreType.DMA((8,)),
        ],
        compiler_params=pltpu.CompilerParams(
            collective_id=0, has_side_effects=True, vmem_limit_bytes=VMEM_BYTES
        ),
    )(
        vis,
        wp.reshape(8, 256, 512),
        bias,
        txt.reshape(8, 2, 64, 512),
        gain.reshape(1, 512),
        kw,
        grp,
        off,
    )


def solution(mesh):
    in_specs = (
        P(("section", "group"), "tp"),
        P("group", "tp"),
        P("tp"),
        P(("section", "group"), "tp"),
        P("tp"),
        P("tp", None),
        P(),
        P(),
    )
    out_specs = P(("section", "group", "tp"), None)
    return jax.shard_map(
        on_device, mesh=mesh, in_specs=in_specs, out_specs=out_specs, check_vma=False
    )
```

```python
import jax
import jax.numpy as jnp
from jax import lax
from jax.experimental import pallas as pl
from jax.experimental.pallas import tpu as pltpu
from jax.sharding import PartitionSpec as P

MESH = pl.DeviceIdType.MESH
D = 8192
KV = 1024
PAD = 128
WIDE = KV + PAD
EPS = 1e-05
BIG = 1.9e19
F32 = jnp.float32
BF16 = jnp.bfloat16
NEAR = 512
SEMS = 144
VMEM_BYTES = 62 * 1024 * 1024


def dot(a, b):
    return jnp.dot(a, b, preferred_element_type=F32)


def three_parts(v):
    lane = lax.broadcasted_iota(jnp.int32, (v.shape[0], PAD), 1)
    hi = v.astype(BF16).astype(F32)
    rest = jnp.where(hi < jnp.inf, v - hi, 0.0)
    mid = rest.astype(BF16).astype(F32)
    low = rest - mid
    parts = jnp.where(lane == 0, hi, jnp.where(lane == 1, mid, jnp.where(lane == 2, low, 0.0)))
    return parts.astype(BF16)


def inverse_rms(half_sum):
    return 1.0 / jnp.sqrt(half_sum * 2.0 / D + EPS)


def kernel(
    vis, wp, bias_in, txt, gain_in, kw, grp_in, off_in, out,
    bias, gain, grp, off, xb, wb, tv, kwv, tsend, trecv, town, csend, crecv, acc, inear, izsend, izrecv,
    iysend, iyrecv, isend, irecv,
    ikey, dest, asend, fin, ssem, rsem, lsem,
):
    s, g, t = lax.axis_index("section"), lax.axis_index("group"), lax.axis_index("tp")
    y, l = t // 2, t % 2
    other = 1 - l
    partner = 2 * y + other
    up, down = 2 * ((y + 1) % 8) + l, 2 * ((y + 7) % 8) + l
    sib = s + 1 - 2 * (s % 2)
    g_up, g_down, g_far = (g + 1) % 4, (g + 3) % 4, (g + 2) % 4
    s_up, s_down, s_far = (s + 2) % 8, (s + 6) % 8, (s + 4) % 8

    local = []
    pairs = (
        (txt, tv), (kw, kwv), (gain_in, gain), (vis, xb.at[t]), (wp, wb.at[pl.ds(8 * g, 8)]),
        (bias_in, bias), (grp_in, grp), (off_in, off),
    )
    for k, (src, dst) in enumerate(pairs):
        copy = pltpu.make_async_copy(src, dst, lsem.at[k])
        copy.start()
        local.append(copy)

    peers = [{"tp": partner}, {"tp": up}, {"tp": down}, {"group": g_up}, {"group": g_down}]
    peers += [{"section": s_up}, {"section": s_down}, {"section": sib}]
    barrier = pltpu.get_barrier_semaphore()
    for peer in peers:
        pl.semaphore_signal(barrier, inc=1, device_id=peer, device_id_type=MESH)
    pl.semaphore_wait(barrier, len(peers))

    sent = []

    def send(src, dst, **peer):
        k = len(sent)
        copy = pltpu.make_async_remote_copy(
            src_ref=src, dst_ref=dst, send_sem=ssem.at[k], recv_sem=rsem.at[k],
            device_id=peer, device_id_type=MESH,
        )
        copy.start()
        sent.append(copy)
        return k, peer

    def pass_on(ref, **peer):
        return send(ref, ref, **peer)

    def arrive(handle, dst):
        k, peer = handle
        pltpu.make_async_remote_copy(
            src_ref=dst, dst_ref=dst, send_sem=ssem.at[k], recv_sem=rsem.at[k],
            device_id=peer, device_id_type=MESH,
        ).wait_recv()

    lo, hi = pl.ds(0, 128), pl.ds(128, 128)

    def block(k, lane):
        return xb.at[2 * ((y + k + 8) % 8) + lane]

    lanes = (l, other)
    halves = (lo, hi)
    right, left = {}, {}

    def ring_start(q, half):
        ref = xb.at[t, halves[half]]
        if q == 0:
            src = vis.at[halves[half]]
        else:
            arrive(to_partner[half], xb.at[partner, halves[half]])
            src = ref = xb.at[partner, halves[half]]
        right[q, half] = send(src, ref, tp=up)
        left[q, half] = send(src, ref, tp=down)

    def ring_on(q, half, step):
        a, b = block(-step, lanes[q]).at[halves[half]], block(step, lanes[q]).at[halves[half]]
        arrive(right[q, half], a)
        if step < 3 or half == 0:
            right[q, half] = pass_on(a, tp=up)
        arrive(left[q, half], b)
        if step < 3 or half == 1:
            left[q, half] = pass_on(b, tp=down)

    def ring_end(q):
        arrive(right[q, 0], block(4, lanes[q]).at[lo])
        arrive(left[q, 1], block(4, lanes[q]).at[hi])

    groups = {"down": g_down, "up": g_up, "far": g_far}

    def piece(h, section):
        return wb.at[8 * (groups[h] if isinstance(h, str) else h) + section]

    along, to_sib = {}, {"down": [], "up": [], "far": []}

    def spread(h, rows, name):
        ref = piece(h, s).at[rows]
        along[name, h] = (pass_on(ref, section=s_up), pass_on(ref, section=s_down))

    def to_core(h, section, rows=pl.ds(0, 256)):
        handle = pass_on(piece(h, section).at[rows], section=sib)
        to_sib[h].append((handle, piece(h, (section + sib - s + 8) % 8).at[rows]))

    def spread_on(h):
        arrive(along["lo", h][0], piece(h, s_down).at[lo])
        end_lo = pass_on(piece(h, s_down).at[lo], section=s_up)
        arrive(along["hi", h][1], piece(h, s_up).at[hi])
        end_hi = pass_on(piece(h, s_up).at[hi], section=s_down)
        arrive(along["hi", h][0], piece(h, s_down).at[hi])
        to_core(h, s_down)
        arrive(along["lo", h][1], piece(h, s_up).at[lo])
        to_core(h, s_up)
        along["end", h] = (end_lo, end_hi)

    def spread_end(h):
        arrive(along["end", h][0], piece(h, s_far).at[lo])
        to_core(h, s_far, lo)
        arrive(along["end", h][1], piece(h, s_far).at[hi])
        to_core(h, s_far, hi)

    ring_start(0, 0)
    ring_start(0, 1)
    z_up, z_down, to_partner = {}, {}, []
    for k, half in enumerate(halves):
        z_up[k] = send(wp.at[s, half], piece(g, s).at[half], group=g_up)
        flip = halves[1 - k]
        z_down[1 - k] = send(wp.at[s, flip], piece(g, s).at[flip], group=g_down)
        to_partner.append(send(vis.at[half], xb.at[t, half], tp=partner))

    for k in range(3):
        local[k].wait()

    def text_part(which, j):
        part = tv[pl.ds(4 * j, 4), which].reshape(256, 512).astype(F32)
        part = jnp.minimum(jnp.maximum(part, -BIG), BIG)
        half = jnp.sum(part * part, axis=1, keepdims=True) * 0.5
        part = part * gain[...]
        coarse = part.astype(BF16)
        fine = (part - coarse.astype(F32)).astype(BF16)
        return dot(coarse, kwv[...]) + dot(fine, kwv[...]), half

    def text_for_partner(j):
        keys, half = text_part(other, j)
        tsend[pl.ds(4 * j, 4), :, :KV] = keys.astype(BF16).reshape(4, 64, KV)
        tsend[pl.ds(4 * j, 4), :, KV:] = three_parts(half).reshape(4, 64, PAD)

    def text_here(j):
        keys, half = text_part(l, j)
        lane = lax.broadcasted_iota(jnp.int32, (256, PAD), 1)
        town[pl.ds(4 * j, 4), :, :KV] = keys.reshape(4, 64, KV)
        town[pl.ds(4 * j, 4), :, KV:] = jnp.where(lane == 0, half, 0.0).reshape(4, 64, PAD)

    text_for_partner(0)
    ring_on(0, 0, 1)
    text_for_partner(1)
    ring_on(0, 1, 1)
    arrive(z_up[0], piece("down", s).at[lo])
    far_lo = pass_on(piece("down", s).at[lo], group=g_up)
    spread("down", lo, "lo")
    arrive(z_down[1], piece("up", s).at[hi])
    far_hi = pass_on(piece("up", s).at[hi], group=g_down)
    spread("up", hi, "hi")
    ring_start(1, 0)
    ring_on(0, 0, 2)
    text_here(0)
    ring_on(0, 1, 2)
    arrive(z_up[1], piece("down", s).at[hi])
    spread("down", hi, "hi")
    to_core("down", s)
    arrive(z_down[0], piece("up", s).at[lo])
    spread("up", lo, "lo")
    to_core("up", s)
    ring_start(1, 1)
    ring_on(0, 0, 3)
    ring_on(0, 1, 3)
    text_here(1)
    arrive(far_lo, piece("far", s).at[lo])
    spread("far", lo, "lo")
    arrive(far_hi, piece("far", s).at[hi])
    spread("far", hi, "hi")
    to_core("far", s)
    text_z = {}
    for k in (4, 5, 3, 6, 2, 7, 1, 0):
        window = (y + k) % 8
        text_z[k] = send(tsend.at[window], trecv.at[window], tp=partner)
    ring_on(1, 0, 1)
    ring_on(1, 1, 1)
    spread_on("down")
    spread_on("up")
    ring_on(1, 0, 2)
    ring_on(1, 1, 2)
    spread_on("far")
    ring_on(1, 0, 3)
    ring_on(1, 1, 3)
    spread_end("down")
    spread_end("up")
    spread_end("far")

    chain = {}

    def chain_on(step):
        for way, (to, sign) in enumerate(((up, 1), (down, 7))):
            rows = pl.ds(0, 64)
            if step == 1:
                rows = pl.ds(32 * way, 32)
            k = sign * (5 - step) % 8
            window = (y + k) % 8
            if step > 1 or way == 0:
                arrive(text_z[k], trecv.at[window])
            total = town[window, rows] + trecv[window, rows].astype(F32)
            if step == 2:
                first = pl.ds(32 * way, 32)
                arrive(chain[way], crecv.at[way, 0, first])
                came = crecv[way, 0, first].astype(F32)
                empty = jnp.zeros_like(came)
                total += jnp.concatenate([came, empty] if way == 0 else [empty, came], axis=0)
            elif step > 2:
                arrive(chain[way], crecv.at[way, step - 2])
                total += crecv[way, step - 2].astype(F32)
            csend[way, step - 1, rows, :KV] = total[:, :KV].astype(BF16)
            csend[way, step - 1, rows, KV:] = three_parts(
                jnp.sum(total[:, KV:], axis=1, keepdims=True)
            )
            chain[way] = send(
                csend.at[way, step - 1, rows], crecv.at[way, step - 1, rows], tp=to
            )

    chain_on(1)

    for k in range(3, 8):
        local[k].wait()

    def project(k):
        w = wb[pl.ds(4 * k, 4)].reshape(1024, 512)
        return dot(xb[2 * k], w[:512]) + dot(xb[2 * k + 1], w[512:])

    def project_group(h):
        @pl.loop(0, 2)
        def _(j):
            @pl.when(2 * h + j != (y + 4) % 8)
            def _():
                acc[...] += project(2 * h + j)

    acc[...] = jnp.zeros_like(acc) + bias[...].astype(F32).reshape(1, 512)
    project_group(g)
    for h in ("down", "up", "far"):
        for handle, ref in to_sib[h]:
            arrive(handle, ref)
        if h == "far":
            chain_on(2)
        project_group(groups[h])
    ring_end(0)
    ring_end(1)
    image = (acc[...] + project((y + 4) % 8)).astype(BF16)

    own_start = off[4 * s + g]
    turned = (lax.broadcasted_iota(jnp.int32, (256, 256), 0) - own_start) & 255
    turn = jnp.where(turned == lax.broadcasted_iota(jnp.int32, (256, 256), 1), 1.0, 0.0)
    image = dot(turn.astype(BF16), image)
    half = jnp.sum(image * image, axis=1, keepdims=True) * 0.5
    keys = dot((image * gain[...]).astype(BF16), kwv[...]).astype(BF16)
    inear[...] = keys[:, :NEAR].reshape(8, 2, 16, NEAR)
    izsend[...] = inear[:, other]
    near = send(izsend, izrecv, tp=partner)
    isend[:, :, : KV - NEAR] = keys[:, NEAR:].reshape(16, 16, KV - NEAR)
    isend[:, :, KV - NEAR :] = three_parts(half).reshape(16, 16, PAD)
    parts = [
        send(isend.at[(t + d) % 16], irecv.at[d], tp=(t + d) % 16) for d in range(1, 16)
    ]
    arrive(near, izrecv)
    iysend[...] = (inear[:, l].astype(F32) + izrecv[...].astype(F32)).astype(BF16)
    near = [
        send(iysend.at[(y + d) % 8], iyrecv.at[d], tp=2 * ((y + d) % 8) + l) for d in range(1, 8)
    ]
    first = inear[y, l].astype(F32) + izrecv[y].astype(F32)
    rest = isend[t].astype(F32)
    for d in range(1, 16):
        arrive(parts[d - 1], irecv.at[d])
        rest += irecv[d].astype(F32)
    for d in range(1, 8):
        arrive(near[d - 1], iyrecv.at[d])
        first += iyrecv[d].astype(F32)
    image = jnp.concatenate([first, rest], axis=1)
    scale = inverse_rms(jnp.sum(image[:, KV:], axis=1, keepdims=True))
    ikey[...] = (image[:, :KV] * scale).astype(BF16)
    placed = [send(ikey, dest.at[g], section=s_far, group=(g + d) % 4) for d in range(4)]
    chain_on(3)

    starts = [
        jnp.where(grp[s_far * 4 + k] == g, off[s_far * 4 + k], 1 << 20) for k in range(4)
    ]

    def inside(row, k):
        return (row >= starts[k]) & (row < starts[k] + 256)

    for k in range(4):
        arrive(placed[k], dest.at[(g + 4 - k) % 4])
    base = SEMS - 4
    slot = t % 4
    last = []
    for m in range(4):
        row = lax.broadcasted_iota(jnp.int32, (16, 1), 0) + 256 * m + 16 * t
        chosen = jnp.zeros((16, KV), F32)
        for k in range(4):
            chosen = jnp.where(inside(row, k), dest[k].astype(F32), chosen)
        asend[m] = chosen.astype(BF16)
        target = t // 4 + 4 * m
        copy = pltpu.make_async_remote_copy(
            src_ref=asend.at[m], dst_ref=fin.at[slot], send_sem=ssem.at[base + m],
            recv_sem=rsem.at[base + slot], device_id={"tp": target}, device_id_type=MESH,
        )
        last.append((copy, target))

        @pl.when(target != t)
        def _():
            copy.start()

        @pl.when(target == t)
        def _():
            fin[slot] = asend[m]

    chain_on(4)
    arrive(text_z[0], trecv.at[y])
    text = town[y] + trecv[y].astype(F32)
    for way in range(2):
        arrive(chain[way], crecv.at[way, 3])
        text += crecv[way, 3].astype(F32)
    keys = text[:, :KV] * inverse_rms(jnp.sum(text[:, KV:], axis=1, keepdims=True))
    for j in range(4):
        source = 4 * (t % 4) + j

        @pl.when(source != t)
        def _():
            pltpu.make_async_remote_copy(
                src_ref=fin.at[j], dst_ref=fin.at[j], send_sem=ssem.at[base + j],
                recv_sem=rsem.at[base + j], device_id={"tp": source}, device_id_type=MESH,
            ).wait_recv()

    row = lax.broadcasted_iota(jnp.int32, (64, 1), 0) + 64 * t
    hit = inside(row, 0) | inside(row, 1) | inside(row, 2) | inside(row, 3)
    out[...] = jnp.where(hit, fin[...].reshape(64, KV).astype(F32), keys).astype(BF16)

    for copy in sent:
        copy.wait_send()
    for copy, target in last:

        @pl.when(target != t)
        def _():
            copy.wait_send()


def on_device(vis, wp, bias, txt, gain, kw, grp, off):
    return pl.pallas_call(
        kernel,
        out_shape=jax.ShapeDtypeStruct((64, KV), BF16),
        in_specs=[pl.BlockSpec(memory_space=pl.ANY)] * 8,
        out_specs=pl.BlockSpec(memory_space=pltpu.VMEM),
        scratch_shapes=[
            pltpu.VMEM((512,), BF16),
            pltpu.VMEM((1, 512), F32),
            pltpu.SMEM((32,), jnp.int32),
            pltpu.SMEM((32,), jnp.int32),
            pltpu.VMEM((16, 256, 512), BF16),
            pltpu.VMEM((32, 256, 512), BF16),
            pltpu.VMEM((8, 2, 64, 512), BF16),
            pltpu.VMEM((512, KV), BF16),
            pltpu.VMEM((8, 64, WIDE), BF16),
            pltpu.VMEM((8, 64, WIDE), BF16),
            pltpu.VMEM((8, 64, WIDE), F32),
            pltpu.VMEM((2, 4, 64, WIDE), BF16),
            pltpu.VMEM((2, 4, 64, WIDE), BF16),
            pltpu.VMEM((256, 512), F32),
            pltpu.VMEM((8, 2, 16, NEAR), BF16),
            pltpu.VMEM((8, 16, NEAR), BF16),
            pltpu.VMEM((8, 16, NEAR), BF16),
            pltpu.VMEM((8, 16, NEAR), BF16),
            pltpu.VMEM((8, 16, NEAR), BF16),
            pltpu.VMEM((16, 16, WIDE - NEAR), BF16),
            pltpu.VMEM((16, 16, WIDE - NEAR), BF16),
            pltpu.VMEM((16, KV), BF16),
            pltpu.VMEM((4, 16, KV), BF16),
            pltpu.VMEM((4, 16, KV), BF16),
            pltpu.VMEM((4, 16, KV), BF16),
            pltpu.SemaphoreType.DMA((SEMS,)),
            pltpu.SemaphoreType.DMA((SEMS,)),
            pltpu.SemaphoreType.DMA((8,)),
        ],
        compiler_params=pltpu.CompilerParams(
            collective_id=0, has_side_effects=True, vmem_limit_bytes=VMEM_BYTES
        ),
    )(
        vis,
        wp.reshape(8, 256, 512),
        bias,
        txt.reshape(8, 2, 64, 512),
        gain.reshape(1, 512),
        kw,
        grp,
        off,
    )


def solution(mesh):
    in_specs = (
        P(("section", "group"), "tp"),
        P("group", "tp"),
        P("tp"),
        P(("section", "group"), "tp"),
        P("tp"),
        P("tp", None),
        P(),
        P(),
    )
    out_specs = P(("section", "group", "tp"), None)
    return jax.shard_map(
        on_device, mesh=mesh, in_specs=in_specs, out_specs=out_specs, check_vma=False
    )
```

```python
import jax
import jax.numpy as jnp
from jax import lax
from jax.experimental import pallas as pl
from jax.experimental.pallas import tpu as pltpu
from jax.sharding import PartitionSpec as P

MESH = pl.DeviceIdType.MESH
D = 8192
KV = 1024
PAD = 128
WIDE = KV + PAD
EPS = 1e-05
BIG = 1.9e19
F32 = jnp.float32
BF16 = jnp.bfloat16
NEAR = 512
SEMS = 144
VMEM_BYTES = 62 * 1024 * 1024


def dot(a, b):
    return jnp.dot(a, b, preferred_element_type=F32)


def three_parts(v):
    lane = lax.broadcasted_iota(jnp.int32, (v.shape[0], PAD), 1)
    hi = v.astype(BF16).astype(F32)
    rest = jnp.where(hi < jnp.inf, v - hi, 0.0)
    mid = rest.astype(BF16).astype(F32)
    low = rest - mid
    parts = jnp.where(lane == 0, hi, jnp.where(lane == 1, mid, jnp.where(lane == 2, low, 0.0)))
    return parts.astype(BF16)


def inverse_rms(half_sum):
    return 1.0 / jnp.sqrt(half_sum * 2.0 / D + EPS)


def kernel(
    vis, wp, bias_in, txt, gain_in, kw, grp_in, off_in, out,
    bias, gain, grp, off, xb, wb, tv, kwv, ssend, srecv, tsend, trecv, town, csend, crecv, acc, inear, izsend, izrecv,
    iysend, iyrecv, isend, irecv,
    ikey, dest, asend, fin, ssem, rsem, lsem,
):
    s, g, t = lax.axis_index("section"), lax.axis_index("group"), lax.axis_index("tp")
    y, l = t // 2, t % 2
    other = 1 - l
    partner = 2 * y + other
    up, down = 2 * ((y + 1) % 8) + l, 2 * ((y + 7) % 8) + l
    sib = s + 1 - 2 * (s % 2)
    g_up, g_down, g_far = (g + 1) % 4, (g + 3) % 4, (g + 2) % 4
    s_up, s_down, s_far = (s + 2) % 8, (s + 6) % 8, (s + 4) % 8

    local = []
    pairs = (
        (txt, tv), (kw, kwv), (gain_in, gain), (vis, xb.at[t]), (wp, wb.at[pl.ds(8 * g, 8)]),
        (bias_in, bias), (grp_in, grp), (off_in, off),
    )
    for k, (src, dst) in enumerate(pairs):
        copy = pltpu.make_async_copy(src, dst, lsem.at[k])
        copy.start()
        local.append(copy)

    peers = [{"tp": partner}, {"tp": up}, {"tp": down}, {"group": g_up}, {"group": g_down}]
    peers += [{"section": s_up}, {"section": s_down}, {"section": sib}]
    barrier = pltpu.get_barrier_semaphore()
    for peer in peers:
        pl.semaphore_signal(barrier, inc=1, device_id=peer, device_id_type=MESH)
    pl.semaphore_wait(barrier, len(peers))

    sent = []

    def send(src, dst, **peer):
        k = len(sent)
        copy = pltpu.make_async_remote_copy(
            src_ref=src, dst_ref=dst, send_sem=ssem.at[k], recv_sem=rsem.at[k],
            device_id=peer, device_id_type=MESH,
        )
        copy.start()
        sent.append(copy)
        return k, peer

    def pass_on(ref, **peer):
        return send(ref, ref, **peer)

    def arrive(handle, dst):
        k, peer = handle
        pltpu.make_async_remote_copy(
            src_ref=dst, dst_ref=dst, send_sem=ssem.at[k], recv_sem=rsem.at[k],
            device_id=peer, device_id_type=MESH,
        ).wait_recv()

    lo, hi = pl.ds(0, 128), pl.ds(128, 128)

    def block(k, lane):
        return xb.at[2 * ((y + k + 8) % 8) + lane]

    lanes = (l, other)
    halves = (lo, hi)
    right, left = {}, {}

    def ring_start(q, half):
        ref = xb.at[t, halves[half]]
        if q == 0:
            src = vis.at[halves[half]]
        else:
            arrive(to_partner[half], xb.at[partner, halves[half]])
            src = ref = xb.at[partner, halves[half]]
        right[q, half] = send(src, ref, tp=up)
        left[q, half] = send(src, ref, tp=down)

    def ring_on(q, half, step):
        a, b = block(-step, lanes[q]).at[halves[half]], block(step, lanes[q]).at[halves[half]]
        arrive(right[q, half], a)
        if step < 3 or half == 0:
            right[q, half] = pass_on(a, tp=up)
        arrive(left[q, half], b)
        if step < 3 or half == 1:
            left[q, half] = pass_on(b, tp=down)

    def ring_end(q):
        arrive(right[q, 0], block(4, lanes[q]).at[lo])
        arrive(left[q, 1], block(4, lanes[q]).at[hi])

    groups = {"down": g_down, "up": g_up, "far": g_far}

    def piece(h, section):
        return wb.at[8 * (groups[h] if isinstance(h, str) else h) + section]

    along, to_sib = {}, {"down": [], "up": [], "far": []}

    def spread(h, rows, name):
        ref = piece(h, s).at[rows]
        along[name, h] = (pass_on(ref, section=s_up), pass_on(ref, section=s_down))

    def to_core(h, section, rows=pl.ds(0, 256)):
        handle = pass_on(piece(h, section).at[rows], section=sib)
        to_sib[h].append((handle, piece(h, (section + sib - s + 8) % 8).at[rows]))

    def spread_on(h):
        arrive(along["lo", h][0], piece(h, s_down).at[lo])
        end_lo = pass_on(piece(h, s_down).at[lo], section=s_up)
        arrive(along["hi", h][1], piece(h, s_up).at[hi])
        end_hi = pass_on(piece(h, s_up).at[hi], section=s_down)
        arrive(along["hi", h][0], piece(h, s_down).at[hi])
        to_core(h, s_down)
        arrive(along["lo", h][1], piece(h, s_up).at[lo])
        to_core(h, s_up)
        along["end", h] = (end_lo, end_hi)

    def spread_end(h):
        arrive(along["end", h][0], piece(h, s_far).at[lo])
        to_core(h, s_far, lo)
        arrive(along["end", h][1], piece(h, s_far).at[hi])
        to_core(h, s_far, hi)

    ring_start(0, 0)
    ring_start(0, 1)
    z_up, z_down = {}, {}

    def weights_out(k):
        half, flip = halves[k], halves[1 - k]
        z_up[k] = send(wp.at[s, half], piece(g, s).at[half], group=g_up)
        z_down[1 - k] = send(wp.at[s, flip], piece(g, s).at[flip], group=g_down)

    def features_out(k):
        return send(vis.at[halves[k]], xb.at[t, halves[k]], tp=partner)

    to_partner = [features_out(0)]
    weights_out(0)

    for k in range(3):
        local[k].wait()

    def text_part(which, j):
        part = tv[pl.ds(4 * j, 4), which].reshape(256, 512).astype(F32)
        part = jnp.minimum(jnp.maximum(part, -BIG), BIG)
        half = jnp.sum(part * part, axis=1, keepdims=True) * 0.5
        part = part * gain[...]
        coarse = part.astype(BF16)
        fine = (part - coarse.astype(F32)).astype(BF16)
        return dot(coarse, kwv[...]) + dot(fine, kwv[...]), half

    def text_for_partner(j):
        keys, half = text_part(other, j)
        tsend[pl.ds(4 * j, 4)] = keys.astype(BF16).reshape(4, 64, KV)
        lane = lax.broadcasted_iota(jnp.int32, (64, PAD), 1)
        squares = jnp.zeros((64, PAD), F32) if j == 0 else ssend[...]
        for i in range(4):
            squares = jnp.where(lane == 4 * j + i, half[64 * i : 64 * i + 64], squares)
        ssend[...] = squares

    def text_here(j):
        keys, half = text_part(l, j)
        lane = lax.broadcasted_iota(jnp.int32, (256, PAD), 1)
        town[pl.ds(4 * j, 4), :, :KV] = keys.reshape(4, 64, KV)
        town[pl.ds(4 * j, 4), :, KV:] = jnp.where(lane == 0, half, 0.0).reshape(4, 64, PAD)

    text_for_partner(0)
    left_device = (z_up[0][0], z_down[1][0])
    for k in left_device:
        sent[k].wait_send()
    to_partner.append(features_out(1))
    ring_on(0, 0, 1)
    weights_out(1)
    text_for_partner(1)
    ring_on(0, 1, 1)
    arrive(z_up[0], piece("down", s).at[lo])
    far_lo = pass_on(piece("down", s).at[lo], group=g_up)
    spread("down", lo, "lo")
    arrive(z_down[1], piece("up", s).at[hi])
    far_hi = pass_on(piece("up", s).at[hi], group=g_down)
    spread("up", hi, "hi")
    ring_start(1, 0)
    ring_on(0, 0, 2)
    text_here(0)
    ring_on(0, 1, 2)
    arrive(z_up[1], piece("down", s).at[hi])
    spread("down", hi, "hi")
    to_core("down", s)
    arrive(z_down[0], piece("up", s).at[lo])
    spread("up", lo, "lo")
    to_core("up", s)
    ring_start(1, 1)
    ring_on(0, 0, 3)
    ring_on(0, 1, 3)
    text_here(1)
    arrive(far_lo, piece("far", s).at[lo])
    spread("far", lo, "lo")
    arrive(far_hi, piece("far", s).at[hi])
    spread("far", hi, "hi")
    to_core("far", s)
    text_z = {}
    squares_z = send(ssend, srecv, tp=partner)
    for k in (4, 5, 3, 6, 2, 7, 1, 0):
        window = (y + k) % 8
        text_z[k] = send(tsend.at[window], trecv.at[window], tp=partner)
    ring_on(1, 0, 1)
    ring_on(1, 1, 1)
    spread_on("down")
    spread_on("up")
    ring_on(1, 0, 2)
    ring_on(1, 1, 2)
    spread_on("far")
    ring_on(1, 0, 3)
    ring_on(1, 1, 3)
    spread_end("down")
    spread_end("up")
    spread_end("far")

    chain = {}

    def with_partner(window, rows):
        lane = lax.broadcasted_iota(jnp.int32, (rows.size, PAD), 1)
        theirs = jnp.where(lane == window, srecv[rows], 0.0)
        keys = town[window, rows, :KV] + trecv[window, rows].astype(F32)
        return jnp.concatenate([keys, town[window, rows, KV:] + theirs], axis=1)

    def chain_on(step):
        if step == 1:
            arrive(squares_z, srecv)
        for way, (to, sign) in enumerate(((up, 1), (down, 7))):
            rows = pl.ds(0, 64)
            if step == 1:
                rows = pl.ds(32 * way, 32)
            k = sign * (5 - step) % 8
            window = (y + k) % 8
            if step > 1 or way == 0:
                arrive(text_z[k], trecv.at[window])
            total = with_partner(window, rows)
            if step == 2:
                first = pl.ds(32 * way, 32)
                arrive(chain[way], crecv.at[way, 0, first])
                came = crecv[way, 0, first].astype(F32)
                empty = jnp.zeros_like(came)
                total += jnp.concatenate([came, empty] if way == 0 else [empty, came], axis=0)
            elif step > 2:
                arrive(chain[way], crecv.at[way, step - 2])
                total += crecv[way, step - 2].astype(F32)
            csend[way, step - 1, rows, :KV] = total[:, :KV].astype(BF16)
            csend[way, step - 1, rows, KV:] = three_parts(
                jnp.sum(total[:, KV:], axis=1, keepdims=True)
            )
            chain[way] = send(
                csend.at[way, step - 1, rows], crecv.at[way, step - 1, rows], tp=to
            )

    chain_on(1)

    for k in range(3, 8):
        local[k].wait()

    def project(k):
        w = wb[pl.ds(4 * k, 4)].reshape(1024, 512)
        return dot(xb[2 * k], w[:512]) + dot(xb[2 * k + 1], w[512:])

    def project_group(h):
        @pl.loop(0, 2)
        def _(j):
            @pl.when(2 * h + j != (y + 4) % 8)
            def _():
                acc[...] += project(2 * h + j)

    acc[...] = jnp.zeros_like(acc) + bias[...].astype(F32).reshape(1, 512)
    project_group(g)
    for h in ("down", "up", "far"):
        for handle, ref in to_sib[h]:
            arrive(handle, ref)
        if h == "far":
            chain_on(2)
        project_group(groups[h])
    ring_end(0)
    ring_end(1)
    image = (acc[...] + project((y + 4) % 8)).astype(BF16)

    own_start = off[4 * s + g]
    turned = lax.broadcasted_iota(jnp.int32, (256, 256), 0)
    turned = ((turned & 48) << 2) + ((turned >> 6) << 4) + (turned & 15)
    turned = (turned - own_start) & 255
    turn = jnp.where(turned == lax.broadcasted_iota(jnp.int32, (256, 256), 1), 1.0, 0.0)
    image = dot(turn.astype(BF16), image)
    normed = (image * gain[...]).astype(BF16)
    inear[...] = dot(normed, kwv[:, :NEAR]).astype(BF16).reshape(8, 2, 16, NEAR)
    izsend[...] = inear[:, other]
    near = send(izsend, izrecv, tp=partner)
    keys = dot(normed, kwv[:, NEAR:]).astype(BF16)
    isend[:, :, : KV - NEAR] = keys.reshape(16, 16, KV - NEAR)
    half = jnp.sum(image * image, axis=1, keepdims=True) * 0.5
    isend[:, :, KV - NEAR :] = three_parts(half).reshape(16, 16, PAD)
    parts = [
        send(isend.at[(t + d) % 16], irecv.at[d], tp=(t + d) % 16) for d in range(1, 16)
    ]
    arrive(near, izrecv)
    iysend[...] = (inear[:, l].astype(F32) + izrecv[...].astype(F32)).astype(BF16)
    near = [
        send(iysend.at[(y + d) % 8], iyrecv.at[d], tp=2 * ((y + d) % 8) + l) for d in range(1, 8)
    ]
    first = inear[y, l].astype(F32) + izrecv[y].astype(F32)
    rest = isend[t].astype(F32)
    chain_on(3)
    for d in range(1, 16):
        arrive(parts[d - 1], irecv.at[d])
        rest += irecv[d].astype(F32)
    for d in range(1, 8):
        arrive(near[d - 1], iyrecv.at[d])
        first += iyrecv[d].astype(F32)
    image = jnp.concatenate([first, rest], axis=1)
    scale = inverse_rms(jnp.sum(image[:, KV:], axis=1, keepdims=True))
    ikey[...] = (image[:, :KV] * scale).astype(BF16)
    placed = [send(ikey, dest.at[g], section=s_far, group=(g + d) % 4) for d in range(4)]

    chain_on(4)

    starts = [
        jnp.where(grp[s_far * 4 + k] == g, off[s_far * 4 + k], 1 << 20) for k in range(4)
    ]

    def inside(row, k):
        return (row >= starts[k]) & (row < starts[k] + 256)

    for k in range(4):
        arrive(placed[k], dest.at[(g + 4 - k) % 4])
    here = 64 * (t % 4) + 16 * (t // 4)

    def chosen(m):
        row = lax.broadcasted_iota(jnp.int32, (16, 1), 0) + 256 * m + here
        rows = jnp.zeros((16, KV), F32)
        for k in range(4):
            rows = jnp.where(inside(row, k), dest[k].astype(F32), rows)
        return rows.astype(BF16)

    last = []
    for d in range(1, 4):
        target = (t + 4 * d) % 16
        asend[d] = chosen(target // 4)
        last.append(send(asend.at[d], fin.at[t // 4], tp=target))
    fin[t // 4] = chosen(t // 4)
    arrive(text_z[0], trecv.at[y])
    text = with_partner(y, pl.ds(0, 64))
    for way in range(2):
        arrive(chain[way], crecv.at[way, 3])
        text += crecv[way, 3].astype(F32)
    keys = text[:, :KV] * inverse_rms(jnp.sum(text[:, KV:], axis=1, keepdims=True))
    for d in range(1, 4):
        arrive(last[d - 1], fin.at[((t + 16 - 4 * d) % 16) // 4])
    row = lax.broadcasted_iota(jnp.int32, (64, 1), 0) + 64 * t
    hit = inside(row, 0) | inside(row, 1) | inside(row, 2) | inside(row, 3)
    out[...] = jnp.where(hit, fin[...].reshape(64, KV).astype(F32), keys).astype(BF16)

    for k, copy in enumerate(sent):
        if k not in left_device:
            copy.wait_send()


def on_device(vis, wp, bias, txt, gain, kw, grp, off):
    return pl.pallas_call(
        kernel,
        out_shape=jax.ShapeDtypeStruct((64, KV), BF16),
        in_specs=[pl.BlockSpec(memory_space=pl.ANY)] * 8,
        out_specs=pl.BlockSpec(memory_space=pltpu.VMEM),
        scratch_shapes=[
            pltpu.VMEM((512,), BF16),
            pltpu.VMEM((1, 512), F32),
            pltpu.SMEM((32,), jnp.int32),
            pltpu.SMEM((32,), jnp.int32),
            pltpu.VMEM((16, 256, 512), BF16),
            pltpu.VMEM((32, 256, 512), BF16),
            pltpu.VMEM((8, 2, 64, 512), BF16),
            pltpu.VMEM((512, KV), BF16),
            pltpu.VMEM((64, PAD), F32),
            pltpu.VMEM((64, PAD), F32),
            pltpu.VMEM((8, 64, KV), BF16),
            pltpu.VMEM((8, 64, KV), BF16),
            pltpu.VMEM((8, 64, WIDE), F32),
            pltpu.VMEM((2, 4, 64, WIDE), BF16),
            pltpu.VMEM((2, 4, 64, WIDE), BF16),
            pltpu.VMEM((256, 512), F32),
            pltpu.VMEM((8, 2, 16, NEAR), BF16),
            pltpu.VMEM((8, 16, NEAR), BF16),
            pltpu.VMEM((8, 16, NEAR), BF16),
            pltpu.VMEM((8, 16, NEAR), BF16),
            pltpu.VMEM((8, 16, NEAR), BF16),
            pltpu.VMEM((16, 16, WIDE - NEAR), BF16),
            pltpu.VMEM((16, 16, WIDE - NEAR), BF16),
            pltpu.VMEM((16, KV), BF16),
            pltpu.VMEM((4, 16, KV), BF16),
            pltpu.VMEM((4, 16, KV), BF16),
            pltpu.VMEM((4, 16, KV), BF16),
            pltpu.SemaphoreType.DMA((SEMS,)),
            pltpu.SemaphoreType.DMA((SEMS,)),
            pltpu.SemaphoreType.DMA((8,)),
        ],
        compiler_params=pltpu.CompilerParams(
            collective_id=0, has_side_effects=True, vmem_limit_bytes=VMEM_BYTES
        ),
    )(
        vis,
        wp.reshape(8, 256, 512),
        bias,
        txt.reshape(8, 2, 64, 512),
        gain.reshape(1, 512),
        kw,
        grp,
        off,
    )


def solution(mesh):
    in_specs = (
        P(("section", "group"), "tp"),
        P("group", "tp"),
        P("tp"),
        P(("section", "group"), "tp"),
        P("tp"),
        P("tp", None),
        P(),
        P(),
    )
    out_specs = P(("section", "group", "tp"), None)
    return jax.shard_map(
        on_device, mesh=mesh, in_specs=in_specs, out_specs=out_specs, check_vma=False
    )
```

```python
import jax
import jax.numpy as jnp
from jax import lax
from jax.experimental import pallas as pl
from jax.experimental.pallas import tpu as pltpu
from jax.sharding import PartitionSpec as P

MESH = pl.DeviceIdType.MESH
D = 8192
KV = 1024
PAD = 128
WIDE = KV + PAD
EPS = 1e-05
BIG = 1.9e19
F32 = jnp.float32
BF16 = jnp.bfloat16
NEAR = 640
SEMS = 144
VMEM_BYTES = 62 * 1024 * 1024


def dot(a, b):
    return jnp.dot(a, b, preferred_element_type=F32)


def three_parts(v):
    lane = lax.broadcasted_iota(jnp.int32, (v.shape[0], PAD), 1)
    hi = v.astype(BF16).astype(F32)
    rest = jnp.where(hi < jnp.inf, v - hi, 0.0)
    mid = rest.astype(BF16).astype(F32)
    low = rest - mid
    parts = jnp.where(lane == 0, hi, jnp.where(lane == 1, mid, jnp.where(lane == 2, low, 0.0)))
    return parts.astype(BF16)


def inverse_rms(half_sum):
    return 1.0 / jnp.sqrt(half_sum * 2.0 / D + EPS)


def kernel(
    vis, wp, bias_in, txt, gain_in, kw, grp_in, off_in, out,
    bias, gain, grp, off, xb, wb, tv, kwv, ssend, srecv, tsend, trecv, town, csend, crecv, acc, inear, izsend, izrecv,
    iysend, iyrecv, isend, irecv,
    ikey, dest, asend, fin, ssem, rsem, lsem,
):
    s, g, t = lax.axis_index("section"), lax.axis_index("group"), lax.axis_index("tp")
    y, l = t // 2, t % 2
    other = 1 - l
    partner = 2 * y + other
    up, down = 2 * ((y + 1) % 8) + l, 2 * ((y + 7) % 8) + l
    sib = s + 1 - 2 * (s % 2)
    g_up, g_down, g_far = (g + 1) % 4, (g + 3) % 4, (g + 2) % 4
    s_up, s_down, s_far = (s + 2) % 8, (s + 6) % 8, (s + 4) % 8

    local = []
    pairs = (
        (txt, tv), (kw, kwv), (gain_in, gain), (vis, xb.at[t]), (wp, wb.at[pl.ds(8 * g, 8)]),
        (bias_in, bias), (grp_in, grp), (off_in, off),
    )
    for k, (src, dst) in enumerate(pairs):
        copy = pltpu.make_async_copy(src, dst, lsem.at[k])
        copy.start()
        local.append(copy)

    peers = [{"tp": partner}, {"tp": up}, {"tp": down}, {"group": g_up}, {"group": g_down}]
    peers += [{"section": s_up}, {"section": s_down}, {"section": sib}]
    barrier = pltpu.get_barrier_semaphore()
    for peer in peers:
        pl.semaphore_signal(barrier, inc=1, device_id=peer, device_id_type=MESH)
    pl.semaphore_wait(barrier, len(peers))

    sent = []

    def send(src, dst, **peer):
        k = len(sent)
        copy = pltpu.make_async_remote_copy(
            src_ref=src, dst_ref=dst, send_sem=ssem.at[k], recv_sem=rsem.at[k],
            device_id=peer, device_id_type=MESH,
        )
        copy.start()
        sent.append(copy)
        return k, peer

    def pass_on(ref, **peer):
        return send(ref, ref, **peer)

    def arrive(handle, dst):
        k, peer = handle
        pltpu.make_async_remote_copy(
            src_ref=dst, dst_ref=dst, send_sem=ssem.at[k], recv_sem=rsem.at[k],
            device_id=peer, device_id_type=MESH,
        ).wait_recv()

    lo, hi = pl.ds(0, 128), pl.ds(128, 128)

    def block(k, lane):
        return xb.at[2 * ((y + k + 8) % 8) + lane]

    lanes = (l, other)
    halves = (lo, hi)
    right, left = {}, {}

    def ring_start(q, half):
        ref = xb.at[t, halves[half]]
        if q == 0:
            src = vis.at[halves[half]]
        else:
            arrive(to_partner[half], xb.at[partner, halves[half]])
            src = ref = xb.at[partner, halves[half]]
        right[q, half] = send(src, ref, tp=up)
        left[q, half] = send(src, ref, tp=down)

    def ring_on(q, half, step):
        a, b = block(-step, lanes[q]).at[halves[half]], block(step, lanes[q]).at[halves[half]]
        arrive(right[q, half], a)
        if step < 3 or half == 0:
            right[q, half] = pass_on(a, tp=up)
        arrive(left[q, half], b)
        if step < 3 or half == 1:
            left[q, half] = pass_on(b, tp=down)

    def ring_end(q):
        arrive(right[q, 0], block(4, lanes[q]).at[lo])
        arrive(left[q, 1], block(4, lanes[q]).at[hi])

    groups = {"down": g_down, "up": g_up, "far": g_far}

    def piece(h, section):
        return wb.at[8 * (groups[h] if isinstance(h, str) else h) + section]

    along, to_sib = {}, {"down": [], "up": [], "far": []}

    def spread(h, rows, name):
        ref = piece(h, s).at[rows]
        along[name, h] = (pass_on(ref, section=s_up), pass_on(ref, section=s_down))

    def to_core(h, section, rows=pl.ds(0, 256)):
        handle = pass_on(piece(h, section).at[rows], section=sib)
        to_sib[h].append((handle, piece(h, (section + sib - s + 8) % 8).at[rows]))

    def spread_on(h):
        arrive(along["lo", h][0], piece(h, s_down).at[lo])
        end_lo = pass_on(piece(h, s_down).at[lo], section=s_up)
        arrive(along["hi", h][1], piece(h, s_up).at[hi])
        end_hi = pass_on(piece(h, s_up).at[hi], section=s_down)
        arrive(along["hi", h][0], piece(h, s_down).at[hi])
        to_core(h, s_down)
        arrive(along["lo", h][1], piece(h, s_up).at[lo])
        to_core(h, s_up)
        along["end", h] = (end_lo, end_hi)

    def spread_end(h):
        arrive(along["end", h][0], piece(h, s_far).at[lo])
        to_core(h, s_far, lo)
        arrive(along["end", h][1], piece(h, s_far).at[hi])
        to_core(h, s_far, hi)

    ring_start(0, 0)
    ring_start(0, 1)
    z_up, z_down = {}, {}

    def weights_out(k):
        half, flip = halves[k], halves[1 - k]
        z_up[k] = send(wp.at[s, half], piece(g, s).at[half], group=g_up)
        z_down[1 - k] = send(wp.at[s, flip], piece(g, s).at[flip], group=g_down)

    def features_out(k):
        return send(vis.at[halves[k]], xb.at[t, halves[k]], tp=partner)

    to_partner = [features_out(0)]
    weights_out(0)

    for k in range(3):
        local[k].wait()

    def text_part(which, j):
        part = tv[pl.ds(4 * j, 4), which].reshape(256, 512).astype(F32)
        part = jnp.minimum(jnp.maximum(part, -BIG), BIG)
        half = jnp.sum(part * part, axis=1, keepdims=True) * 0.5
        part = part * gain[...]
        coarse = part.astype(BF16)
        fine = (part - coarse.astype(F32)).astype(BF16)
        return dot(coarse, kwv[...]) + dot(fine, kwv[...]), half

    def text_for_partner(j):
        keys, half = text_part(other, j)
        tsend[pl.ds(4 * j, 4)] = keys.astype(BF16).reshape(4, 64, KV)
        lane = lax.broadcasted_iota(jnp.int32, (64, PAD), 1)
        squares = jnp.zeros((64, PAD), F32) if j == 0 else ssend[...]
        for i in range(4):
            squares = jnp.where(lane == 4 * j + i, half[64 * i : 64 * i + 64], squares)
        ssend[...] = squares

    def text_here(j):
        keys, half = text_part(l, j)
        lane = lax.broadcasted_iota(jnp.int32, (256, PAD), 1)
        town[pl.ds(4 * j, 4), :, :KV] = keys.reshape(4, 64, KV)
        town[pl.ds(4 * j, 4), :, KV:] = jnp.where(lane == 0, half, 0.0).reshape(4, 64, PAD)

    text_for_partner(0)
    left_device = (z_up[0][0], z_down[1][0])
    for k in left_device:
        sent[k].wait_send()
    to_partner.append(features_out(1))
    ring_on(0, 0, 1)
    weights_out(1)
    text_for_partner(1)
    ring_on(0, 1, 1)
    arrive(z_up[0], piece("down", s).at[lo])
    far_lo = pass_on(piece("down", s).at[lo], group=g_up)
    spread("down", lo, "lo")
    arrive(z_down[1], piece("up", s).at[hi])
    far_hi = pass_on(piece("up", s).at[hi], group=g_down)
    spread("up", hi, "hi")
    ring_start(1, 0)
    ring_on(0, 0, 2)
    text_here(0)
    ring_on(0, 1, 2)
    arrive(z_up[1], piece("down", s).at[hi])
    spread("down", hi, "hi")
    to_core("down", s)
    arrive(z_down[0], piece("up", s).at[lo])
    spread("up", lo, "lo")
    to_core("up", s)
    ring_start(1, 1)
    ring_on(0, 0, 3)
    ring_on(0, 1, 3)
    text_here(1)
    arrive(far_lo, piece("far", s).at[lo])
    spread("far", lo, "lo")
    arrive(far_hi, piece("far", s).at[hi])
    spread("far", hi, "hi")
    to_core("far", s)
    text_z = {}
    squares_z = send(ssend, srecv, tp=partner)
    for k in (4, 5, 3, 6, 2, 7, 1, 0):
        window = (y + k) % 8
        text_z[k] = send(tsend.at[window], trecv.at[window], tp=partner)
    spread_on("down")
    ring_on(1, 0, 1)
    spread_on("up")
    ring_on(1, 1, 1)
    ring_on(1, 0, 2)
    ring_on(1, 1, 2)
    spread_on("far")
    ring_on(1, 0, 3)
    ring_on(1, 1, 3)
    spread_end("down")
    spread_end("up")
    spread_end("far")

    chain = {}

    def with_partner(window, rows):
        lane = lax.broadcasted_iota(jnp.int32, (rows.size, PAD), 1)
        theirs = jnp.where(lane == window, srecv[rows], 0.0)
        keys = town[window, rows, :KV] + trecv[window, rows].astype(F32)
        return jnp.concatenate([keys, town[window, rows, KV:] + theirs], axis=1)

    def chain_on(step):
        if step == 1:
            arrive(squares_z, srecv)
        for way, (to, sign) in enumerate(((up, 1), (down, 7))):
            rows = pl.ds(0, 64)
            if step == 1:
                rows = pl.ds(32 * way, 32)
            k = sign * (5 - step) % 8
            window = (y + k) % 8
            if step > 1 or way == 0:
                arrive(text_z[k], trecv.at[window])
            total = with_partner(window, rows)
            if step == 2:
                first = pl.ds(32 * way, 32)
                arrive(chain[way], crecv.at[way, 0, first])
                came = crecv[way, 0, first].astype(F32)
                empty = jnp.zeros_like(came)
                total += jnp.concatenate([came, empty] if way == 0 else [empty, came], axis=0)
            elif step > 2:
                arrive(chain[way], crecv.at[way, step - 2])
                total += crecv[way, step - 2].astype(F32)
            csend[way, step - 1, rows, :KV] = total[:, :KV].astype(BF16)
            csend[way, step - 1, rows, KV:] = three_parts(
                jnp.sum(total[:, KV:], axis=1, keepdims=True)
            )
            chain[way] = send(
                csend.at[way, step - 1, rows], crecv.at[way, step - 1, rows], tp=to
            )

    chain_on(1)

    for k in range(3, 8):
        local[k].wait()

    def project(k):
        w = wb[pl.ds(4 * k, 4)].reshape(1024, 512)
        return dot(xb[2 * k], w[:512]) + dot(xb[2 * k + 1], w[512:])

    def project_group(h):
        @pl.loop(0, 2)
        def _(j):
            @pl.when(2 * h + j != (y + 4) % 8)
            def _():
                acc[...] += project(2 * h + j)

    acc[...] = jnp.zeros_like(acc) + bias[...].astype(F32).reshape(1, 512)
    project_group(g)
    for h in ("down", "up", "far"):
        for handle, ref in to_sib[h]:
            arrive(handle, ref)
        if h == "up":
            chain_on(2)
        project_group(groups[h])
    ring_end(0)
    ring_end(1)
    image = (acc[...] + project((y + 4) % 8)).astype(BF16)

    own_start = off[4 * s + g]
    turned = lax.broadcasted_iota(jnp.int32, (256, 256), 0)
    turned = ((turned & 48) << 2) + ((turned >> 6) << 4) + (turned & 15)
    turned = (turned - own_start) & 255
    turn = jnp.where(turned == lax.broadcasted_iota(jnp.int32, (256, 256), 1), 1.0, 0.0)
    image = dot(turn.astype(BF16), image)
    normed = (image * gain[...]).astype(BF16)
    inear[...] = dot(normed, kwv[:, :NEAR]).astype(BF16).reshape(8, 2, 16, NEAR)
    izsend[...] = inear[:, other]
    near = send(izsend, izrecv, tp=partner)
    keys = dot(normed, kwv[:, NEAR:]).astype(BF16)
    isend[:, :, : KV - NEAR] = keys.reshape(16, 16, KV - NEAR)
    half = jnp.sum(image * image, axis=1, keepdims=True) * 0.5
    isend[:, :, KV - NEAR :] = three_parts(half).reshape(16, 16, PAD)
    parts = [
        send(isend.at[(t + d) % 16], irecv.at[d], tp=(t + d) % 16) for d in range(1, 16)
    ]
    arrive(near, izrecv)
    iysend[...] = (inear[:, l].astype(F32) + izrecv[...].astype(F32)).astype(BF16)
    near = [
        send(iysend.at[(y + d) % 8], iyrecv.at[d], tp=2 * ((y + d) % 8) + l) for d in range(1, 8)
    ]
    first = inear[y, l].astype(F32) + izrecv[y].astype(F32)
    rest = isend[t].astype(F32)
    chain_on(3)
    for d in range(1, 16):
        arrive(parts[d - 1], irecv.at[d])
        rest += irecv[d].astype(F32)
    for d in range(1, 8):
        arrive(near[d - 1], iyrecv.at[d])
        first += iyrecv[d].astype(F32)
    image = jnp.concatenate([first, rest], axis=1)
    scale = inverse_rms(jnp.sum(image[:, KV:], axis=1, keepdims=True))
    ikey[...] = (image[:, :KV] * scale).astype(BF16)
    placed = [send(ikey, dest.at[g], section=s_far, group=(g + d) % 4) for d in range(4)]

    chain_on(4)

    starts = [
        jnp.where(grp[s_far * 4 + k] == g, off[s_far * 4 + k], 1 << 20) for k in range(4)
    ]

    def inside(row, k):
        return (row >= starts[k]) & (row < starts[k] + 256)

    for k in range(4):
        arrive(placed[k], dest.at[(g + 4 - k) % 4])
    here = 64 * (t % 4) + 16 * (t // 4)

    def chosen(m):
        row = lax.broadcasted_iota(jnp.int32, (16, 1), 0) + 256 * m + here
        rows = jnp.zeros((16, KV), F32)
        for k in range(4):
            rows = jnp.where(inside(row, k), dest[k].astype(F32), rows)
        return rows.astype(BF16)

    last = []
    for d in range(1, 4):
        target = (t + 4 * d) % 16
        asend[d] = chosen(target // 4)
        last.append(send(asend.at[d], fin.at[t // 4], tp=target))
    fin[t // 4] = chosen(t // 4)
    arrive(text_z[0], trecv.at[y])
    text = with_partner(y, pl.ds(0, 64))
    for way in range(2):
        arrive(chain[way], crecv.at[way, 3])
        text += crecv[way, 3].astype(F32)
    keys = text[:, :KV] * inverse_rms(jnp.sum(text[:, KV:], axis=1, keepdims=True))
    for d in range(1, 4):
        arrive(last[d - 1], fin.at[((t + 16 - 4 * d) % 16) // 4])
    row = lax.broadcasted_iota(jnp.int32, (64, 1), 0) + 64 * t
    hit = inside(row, 0) | inside(row, 1) | inside(row, 2) | inside(row, 3)
    out[...] = jnp.where(hit, fin[...].reshape(64, KV).astype(F32), keys).astype(BF16)

    for k, copy in enumerate(sent):
        if k not in left_device:
            copy.wait_send()


def on_device(vis, wp, bias, txt, gain, kw, grp, off):
    return pl.pallas_call(
        kernel,
        out_shape=jax.ShapeDtypeStruct((64, KV), BF16),
        in_specs=[pl.BlockSpec(memory_space=pl.ANY)] * 8,
        out_specs=pl.BlockSpec(memory_space=pltpu.VMEM),
        scratch_shapes=[
            pltpu.VMEM((512,), BF16),
            pltpu.VMEM((1, 512), F32),
            pltpu.SMEM((32,), jnp.int32),
            pltpu.SMEM((32,), jnp.int32),
            pltpu.VMEM((16, 256, 512), BF16),
            pltpu.VMEM((32, 256, 512), BF16),
            pltpu.VMEM((8, 2, 64, 512), BF16),
            pltpu.VMEM((512, KV), BF16),
            pltpu.VMEM((64, PAD), F32),
            pltpu.VMEM((64, PAD), F32),
            pltpu.VMEM((8, 64, KV), BF16),
            pltpu.VMEM((8, 64, KV), BF16),
            pltpu.VMEM((8, 64, WIDE), F32),
            pltpu.VMEM((2, 4, 64, WIDE), BF16),
            pltpu.VMEM((2, 4, 64, WIDE), BF16),
            pltpu.VMEM((256, 512), F32),
            pltpu.VMEM((8, 2, 16, NEAR), BF16),
            pltpu.VMEM((8, 16, NEAR), BF16),
            pltpu.VMEM((8, 16, NEAR), BF16),
            pltpu.VMEM((8, 16, NEAR), BF16),
            pltpu.VMEM((8, 16, NEAR), BF16),
            pltpu.VMEM((16, 16, WIDE - NEAR), BF16),
            pltpu.VMEM((16, 16, WIDE - NEAR), BF16),
            pltpu.VMEM((16, KV), BF16),
            pltpu.VMEM((4, 16, KV), BF16),
            pltpu.VMEM((4, 16, KV), BF16),
            pltpu.VMEM((4, 16, KV), BF16),
            pltpu.SemaphoreType.DMA((SEMS,)),
            pltpu.SemaphoreType.DMA((SEMS,)),
            pltpu.SemaphoreType.DMA((8,)),
        ],
        compiler_params=pltpu.CompilerParams(
            collective_id=0, has_side_effects=True, vmem_limit_bytes=VMEM_BYTES
        ),
    )(
        vis,
        wp.reshape(8, 256, 512),
        bias,
        txt.reshape(8, 2, 64, 512),
        gain.reshape(1, 512),
        kw,
        grp,
        off,
    )


def solution(mesh):
    in_specs = (
        P(("section", "group"), "tp"),
        P("group", "tp"),
        P("tp"),
        P(("section", "group"), "tp"),
        P("tp"),
        P("tp", None),
        P(),
        P(),
    )
    out_specs = P(("section", "group", "tp"), None)
    return jax.shard_map(
        on_device, mesh=mesh, in_specs=in_specs, out_specs=out_specs, check_vma=False
    )
```
